256 devices in a mesh: batch: 16 (over z_lo, x), tok: 8 (over y, z_hi), grp: 2 (over core).
Axes of the slice: x: 4, y: 4, z: 8 (z_hi: 2, z_lo: 4; z = z_hi * 4 + z_lo), core: 2. Of those that a mesh axis runs over, the one named last changes fastest.
Arguments:
- hidden: bfloat16 [32, 2048, 2432], P('batch', ('tok', 'grp')), may hold values from -6 to 6
- shift: float32 [32, 2432], P('batch'), may hold values from -3 to 3
- scale: float32 [32, 2432], P('batch'), may hold values from -3 to 3
- out_weight: bfloat16 [2432, 64], replicated, may hold values from -0.125 to 0.125
- noisy_latent: float32 [32, 64, 2048], P('batch', ('tok', 'grp')), may hold values from -16 to 16
- timestep: int32 [32], P('batch'), may hold values from 0 to 999
- in_kernel: bfloat16 [3, 3, 16, 512], replicated, may hold values from -0.5 to 0.5
- in_bias: float32 [512], replicated, may hold values from -4 to 4
- norm_gain: float32 [512], replicated, may hold values from 0.1 to 1.9
- norm_bias: float32 [512], replicated, may hold values from -3 to 3
- mid_kernel: bfloat16 [3, 3, 512, 512], replicated, may hold values from -0.09375 to 0.09375
- mid_bias: float32 [512], replicated, may hold values from -3 to 3
- rgb_weight: bfloat16 [512, 3], replicated, may hold values from -0.25 to 0.25
- clip_weight: bfloat16 [512, 1024], replicated, may hold values from -0.25 to 0.25
- text_embed: float32 [32, 1024], P('batch'), may hold values from -6 to 6
- slab_map: int32 [32, 16], P('batch', ('tok', 'grp')), may hold values from 0 to 15, each once within a row
Outputs:
- hidden_grad: bfloat16 [32, 2048, 2432], P('batch', ('tok', 'grp'))
- weight_grad: float32 [2432, 64], P(('batch', 'tok'))
- reward: float32 [32], P('batch')
- placed_pixels: float32 [32, 16, 4, 384], P('batch', ('tok', 'grp'))
The draws below stay inside these ranges and needn't reach their ends.
Inputs may be any that keep to these rules, and one draw needn't show every extreme that they name: Each row of slab_map is a permutation of 0 to 15.
All inputs are finite; a program needn't handle non-finite values.
Results may differ from the reference program's by a relative error of at most 0.014.
Values may be sent and summed in bfloat16 or wider, within the bound.
A program may use at most 128 MiB of HBM per device.

```python
import math
import jax
import jax.numpy as jnp
from jax import lax

D = 2432
LAT_CH = 16
VAE_CH = 512
GROUPS = 32
EMBED = 1024
PCOLS = 64
BATCH = 32
N_SLAB = 16
TOKENS = 2048
SLAB_ROWS = 4
LROWS = 64
LCOLS = 128


def draw_noisy_latent(key, part):
    key = jax.random.fold_in(key, 11)
    first_key = jax.random.fold_in(key, 0)
    row_pos = jnp.arange(LROWS, dtype=jnp.float32) / max(LROWS - 1, 1)
    ramp = jnp.exp(row_pos * math.log(3.0))
    base = jnp.clip(jax.random.normal(first_key, (BATCH, LROWS, LCOLS * LAT_CH), jnp.float32), -4.0, 4.0)
    return base * ramp[None, :, None]


def plant(values, own_key, smallest, high):
    place = [jax.random.randint(jax.random.fold_in(own_key, axis), (), 0, length) for axis, length in enumerate(values.shape)]
    longest = values.shape.index(max(values.shape))
    beside = place[:longest] + [(place[longest] + 1) % values.shape[longest]] + place[longest + 1:]
    return values.at[tuple(place)].set(smallest).at[tuple(beside)].set(high)


def levels(rng, dims, pieces, low, top_value):
    def one(position, parts):
        steps = jax.random.uniform(jax.random.fold_in(jax.random.fold_in(rng, 6), position), (parts,), jnp.float32, low / len(pieces), top_value / len(pieces))
        return jnp.repeat(jnp.exp(steps), dims[position] // parts).reshape((-1,) + (1,) * (len(dims) - position - 1))

    factor_of = one(*pieces[0])
    for cut in pieces[1:]:
        factor_of = factor_of * one(*cut)
    return factor_of


def centred(rng, extent, deviation, most, cuts=(), held_as=jnp.bfloat16):
    level = levels(rng, extent, cuts, -0.22, 0.18) if cuts else 1.0
    drawn = jax.random.normal(rng, extent, jnp.float32) * deviation * level
    return jnp.minimum(jnp.maximum(drawn, -most), most).astype(held_as)


def setup_inputs(seed: int = 0) -> dict:
    splits = jax.random.split(jax.random.key(seed), 17)
    hidden = centred(splits[0], (BATCH, TOKENS, D), 1.0, 6.0, ((0, 16), (1, 16)))
    shift = centred(splits[1], (BATCH, D), 0.5, 3.0, ((0, 16),), jnp.float32)
    scale = centred(splits[2], (BATCH, D), 0.5, 3.0, ((0, 16),), jnp.float32)
    out_weight = centred(splits[3], (D, 4 * LAT_CH), D ** -0.5, 0.125)
    noisy_latent = draw_noisy_latent(jax.random.fold_in(splits[16], 71), 0)
    timestep = plant(jax.random.randint(splits[5], (BATCH,), 0, 1000), jax.random.fold_in(splits[5], 1), 0, 999).astype(jnp.int32)
    in_kernel = centred(splits[6], (3, 3, LAT_CH, VAE_CH), (9 * LAT_CH) ** -0.5, 0.5)
    in_bias = centred(splits[7], (VAE_CH,), 1.0, 4.0, (), jnp.float32)
    norm_gain = jnp.clip(1.0 + 0.18 * jax.random.normal(splits[8], (VAE_CH,), jnp.float32), 0.1, 1.9)
    norm_bias = centred(splits[9], (VAE_CH,), 0.5, 3.0, (), jnp.float32)
    mid_kernel = centred(splits[10], (3, 3, VAE_CH, VAE_CH), (9 * VAE_CH) ** -0.5, 0.09375)
    mid_bias = centred(splits[11], (VAE_CH,), 0.5, 3.0, (), jnp.float32)
    rgb_weight = centred(splits[12], (VAE_CH, 3), VAE_CH ** -0.5, 0.25)
    clip_weight = centred(splits[13], (VAE_CH, EMBED), VAE_CH ** -0.5, 0.25)
    text_embed = centred(splits[14], (BATCH, EMBED), 1.0, 6.0, ((0, 16),), jnp.float32)
    slab_map = jax.vmap(lambda own: jax.random.permutation(own, N_SLAB))(jax.random.split(splits[15], BATCH)).reshape((BATCH, N_SLAB)).astype(jnp.int32)
    return dict(hidden=hidden, shift=shift, scale=scale, out_weight=out_weight, noisy_latent=noisy_latent, timestep=timestep, in_kernel=in_kernel, in_bias=in_bias, norm_gain=norm_gain, norm_bias=norm_bias, mid_kernel=mid_kernel, mid_bias=mid_bias, rgb_weight=rgb_weight, clip_weight=clip_weight, text_embed=text_embed, slab_map=slab_map)


latent_scale = 1.5305
latent_shift = 0.0609
reward_weight = 16.0
epsilon = 1e-06

def noise_level(timestep):
    fraction = (timestep.astype(jnp.float32) + 1.0) / 1000.0
    return 3.0 * fraction / (1.0 + 2.0 * fraction)

def silu_slope(values):
    sigmoid = jax.nn.sigmoid(values)
    return sigmoid * (1.0 + values * (1.0 - sigmoid))

def convolve(padded, kernel):
    return lax.conv_general_dilated(padded.astype(jnp.float32), kernel.astype(jnp.float32), (1, 1), ((0, 0), (1, 1)), dimension_numbers=('NHWC', 'HWIO', 'NHWC'), precision=lax.Precision.HIGHEST)

def transposed(kernel):
    return jnp.transpose(jnp.flip(kernel, (0, 1)), (0, 1, 3, 2))

def pad_rows(padded):
    return jnp.pad(padded, ((0, 0), (1, 1), (0, 0), (0, 0)))

def decode_image(latent, text_vector, in_kernel, in_bias, norm_gain, norm_bias, mid_kernel, mid_bias, rgb_weight, clip_weight):
    cells = LROWS * LCOLS
    width_group = VAE_CH // GROUPS
    group_count = cells * width_group
    first_out = convolve(pad_rows(latent.reshape(1, LROWS, LCOLS, LAT_CH)), in_kernel) + in_bias
    grouped = first_out.reshape(cells, GROUPS, width_group)
    group_mean = lax.optimization_barrier(jnp.sum(grouped, axis=(0, 2))) / group_count
    squares = lax.optimization_barrier(jnp.sum(grouped * grouped, axis=(0, 2))) / group_count
    inverse = lax.rsqrt(squares - group_mean * group_mean + epsilon)
    grouped_norm = (grouped - group_mean[None, :, None]) * inverse[None, :, None]
    shaped = grouped_norm.reshape(1, LROWS, LCOLS, VAE_CH) * norm_gain + norm_bias
    act_one = jax.nn.silu(shaped).astype(jnp.bfloat16)
    second = convolve(pad_rows(act_one), mid_kernel) + mid_bias
    act_two = jax.nn.silu(second)
    decoded = jnp.dot(act_two.astype(jnp.bfloat16).reshape(cells, VAE_CH), rgb_weight, preferred_element_type=jnp.float32).reshape(LROWS, LCOLS * 3)
    pooled = (lax.optimization_barrier(jnp.sum(act_two, axis=(0, 1, 2))) / cells).astype(jnp.bfloat16)
    feature = jnp.dot(pooled[None, :], clip_weight, preferred_element_type=jnp.float32)[0]
    norm_feature = jnp.sqrt(jnp.sum(feature * feature) + epsilon)
    norm_text = jnp.sqrt(jnp.sum(text_vector * text_vector) + epsilon)
    reward = jnp.sum(feature * text_vector) / (norm_feature * norm_text)
    grad_feature = (reward_weight * (text_vector / (norm_feature * norm_text) - reward * feature / (norm_feature * norm_feature))).astype(jnp.bfloat16)
    grad_act = jnp.dot(grad_feature[None, :], clip_weight.T, preferred_element_type=jnp.float32)[0]
    grad_second = (grad_act * silu_slope(second)).astype(jnp.bfloat16)
    grad_act_one = convolve(pad_rows(grad_second), transposed(mid_kernel))
    scaled = grad_act_one * silu_slope(shaped) * norm_gain
    grouped_grad = scaled.reshape(cells, GROUPS, width_group)
    total_grad = lax.optimization_barrier(jnp.sum(grouped_grad, axis=(0, 2))) / group_count
    total_cross = lax.optimization_barrier(jnp.sum(grouped_grad * grouped_norm, axis=(0, 2))) / group_count
    grad_first = ((grouped_grad - total_grad[None, :, None] - grouped_norm * total_cross[None, :, None]) * inverse[None, :, None]).reshape(1, LROWS, LCOLS, VAE_CH).astype(jnp.bfloat16)
    grad_latent = convolve(pad_rows(grad_first), transposed(in_kernel)) / latent_scale
    return (decoded, reward, grad_latent.reshape(LROWS, LCOLS * LAT_CH))

def reference(hidden, shift, scale, out_weight, noisy_latent, timestep, in_kernel, in_bias, norm_gain, norm_bias, mid_kernel, mid_bias, rgb_weight, clip_weight, text_embed, slab_map):
    token_values = hidden.astype(jnp.float32)
    token_mean = lax.optimization_barrier(jnp.mean(token_values, axis=-1, keepdims=True))
    centered = token_values - token_mean
    inverse = lax.rsqrt(lax.optimization_barrier(jnp.mean(centered * centered, axis=-1, keepdims=True)) + epsilon)
    normalized = centered * inverse
    modulated = (normalized * (1.0 + scale[:, None, :]) + shift[:, None, :]).astype(jnp.bfloat16)
    velocity = jnp.dot(modulated.reshape(-1, D), out_weight, preferred_element_type=jnp.float32)
    velocity = velocity.reshape(BATCH, LROWS // 2, PCOLS, 2, 2, LAT_CH).transpose(0, 1, 3, 2, 4, 5).reshape(BATCH, LROWS, LCOLS * LAT_CH)
    noise_sigma = noise_level(timestep)[:, None, None]
    latent = ((noisy_latent - noise_sigma * velocity) / latent_scale + latent_shift).astype(jnp.bfloat16)

    def one_image(inputs):
        return decode_image(inputs[0], inputs[1], in_kernel, in_bias, norm_gain, norm_bias, mid_kernel, mid_bias, rgb_weight, clip_weight)
    decoded, reward, grad_latent = lax.map(one_image, (latent, text_embed))
    grad_velocity = (-noise_sigma * grad_latent).reshape(BATCH, LROWS // 2, 2, PCOLS, 2, LAT_CH).transpose(0, 1, 3, 2, 4, 5)
    grad_velocity = grad_velocity.reshape(BATCH * TOKENS, 4 * LAT_CH).astype(jnp.bfloat16)
    weight_grad = jnp.dot(modulated.reshape(-1, D).T, grad_velocity, preferred_element_type=jnp.float32) / TOKENS
    grad_modulated = jnp.dot(grad_velocity, out_weight.T, preferred_element_type=jnp.float32).reshape(BATCH, TOKENS, D)
    grad_normal = grad_modulated * (1.0 + scale[:, None, :])
    hidden_grad = (inverse * (grad_normal - lax.optimization_barrier(jnp.mean(grad_normal, axis=-1, keepdims=True)) - normalized * lax.optimization_barrier(jnp.mean(grad_normal * normalized, axis=-1, keepdims=True)))).astype(jnp.bfloat16)
    slab_pixels = decoded.reshape(BATCH, N_SLAB, SLAB_ROWS, LCOLS * 3)
    placed = jnp.take_along_axis(slab_pixels, slab_map[:, :, None, None], axis=1)
    return (hidden_grad, weight_grad, reward, placed)
```

```python
import jax
import jax.numpy as jnp
from jax import lax
from jax.experimental import pallas as pl
from jax.experimental.pallas import tpu as pltpu
from jax.sharding import PartitionSpec as P

D = 2432
CH = 512
EMB = 1024
GROUP_N = 131072.0
CELLS = 8192.0
EPS = 1e-6
LSCALE = 1.5305
LSHIFT = 0.0609
REWARD_W = 16.0
BF = jnp.bfloat16
F32 = jnp.float32
MESH = pl.DeviceIdType.MESH

NT = (((1,), (1,)), ((), ()))


def mm(a, b):
    return jnp.dot(a, b, preferred_element_type=F32)


def mm_nt(a, b):
    return lax.dot_general(a, b, NT, preferred_element_type=F32)


def iota(shape, dim):
    return lax.broadcasted_iota(jnp.int32, shape, dim)


def one_hot(cond):
    return jnp.where(cond, 1.0, 0.0).astype(BF)


def noise_level(step, shape):
    fraction = (jnp.full(shape, step, jnp.int32).astype(F32) + 1.0) / 1000.0
    return 3.0 * fraction / (1.0 + 2.0 * fraction)


def group_total(tile):
    lane = iota(tile.shape, 1)
    for step in (1, 2, 4, 8):
        tile = tile + jnp.where(
            (lane & step) != 0, pltpu.roll(tile, step, 1), pltpu.roll(tile, 128 - step, 1)
        )
    return tile


def kernel(
    time_ref, map_ref,
    hidden_h, shift_h, scale_h, outw_h, noisy_h, ink_h, inb_h, gain_h, nbias_h,
    midk_h, midb_h, rgb_h, clip_h, text_h,
    hg_h, wg_ref, rew_out, pix_out,
    hid, shiftv, scalev, outw, noisy, ink, inb, gain, nbias, midk, midb, rgb, clip, text,
    stat_m, stat_i, mod, modt, modp, wrep, ve, nl, latsend, rbuf, lhs, wb,
    first, act, slope, gsec, wgr, gfc, rowbuf,
    p1, p2, p3, rewb, pixg, gvsend, gvr, wt, s1send, s1recv, s2send, s2recv, hgv, own_tokens,
    load_sem, lat_s, lat_r, ex_s, ex_r, pix_s, pix_r, rew_s, rew_r, mod_s, mod_r,
    gv_s, gv_r, s1_s, s1_r, s2_s, s2_r, out_sem,
):
    bt = lax.axis_index("batch")
    tok = lax.axis_index("tok")
    c = lax.axis_index("grp")
    y, zh = lax.div(tok, 2), lax.rem(tok, 2)
    zl, x = lax.div(bt, 4), lax.rem(bt, 4)
    j = 2 * y + c

    pairs = [
        (outw_h, outw), (scale_h, scalev), (shift_h, shiftv), (hidden_h, hid),
        (noisy_h, noisy), (ink_h, ink), (inb_h, inb), (gain_h, gain), (nbias_h, nbias),
        (midb_h, midb), (rgb_h, rgb), (midk_h, midk), (clip_h, clip), (text_h, text),
    ]
    loads = [
        pltpu.make_async_copy(src, dst, load_sem.at[i]) for i, (src, dst) in enumerate(pairs)
    ]
    for copy in loads:
        copy.start()

    bar = pltpu.get_barrier_semaphore()
    for d in range(1, 16):
        n = lax.rem(tok * 2 + c + d, 16)
        pl.semaphore_signal(
            bar, inc=1, device_id={"tok": lax.div(n, 2), "grp": lax.rem(n, 2)}, device_id_type=MESH
        )
        n = lax.rem(x * 4 + y + d, 16)
        pl.semaphore_signal(
            bar, inc=1,
            device_id={"batch": zl * 4 + lax.div(n, 4), "tok": lax.rem(n, 4) * 2 + zh},
            device_id_type=MESH,
        )
        n = lax.rem((zl * 2 + zh) * 2 + c + d, 16)
        pl.semaphore_signal(
            bar, inc=1,
            device_id={
                "batch": lax.div(n, 4) * 4 + x,
                "tok": y * 2 + lax.rem(lax.div(n, 2), 2),
                "grp": lax.rem(n, 2),
            },
            device_id_type=MESH,
        )

    loads[0].wait()
    k64, j256 = iota((64, 256), 0), iota((64, 256), 1)
    spread = one_hot(((k64 >> 5) == (j256 >> 7)) & ((k64 & 31) == (j256 & 31)))
    wrep[...] = mm(outw[...], spread).astype(BF)

    for copy in loads[1:4]:
        copy.wait()

    def norm_rows(i, carry):
        img, start = lax.div(i, 4), pl.multiple_of(lax.rem(i, 4) * 32, 32)
        flat = pl.multiple_of(i * 32, 32)
        values = hid[img, pl.ds(start, 32), :].astype(F32)
        mean = jnp.sum(values, axis=-1, keepdims=True) / D
        centered = values - mean
        inv = lax.rsqrt(jnp.sum(centered * centered, axis=-1, keepdims=True) / D + EPS)
        stat_m[pl.ds(flat, 32), :] = mean
        stat_i[pl.ds(flat, 32), :] = inv
        gain_row = 1.0 + scalev[pl.ds(img, 1), :]
        mod[pl.ds(flat, 32), :] = (
            centered * inv * gain_row + shiftv[pl.ds(img, 1), :]
        ).astype(BF)
        return carry

    lax.fori_loop(0, 8, norm_rows, 0)
    velocity = mm(mod[...], wrep[...])
    for a in range(2):
        ve[a] = velocity[:, a * 128 : a * 128 + 128]

    loads[4].wait()
    for i in range(2):
        for b in range(16):
            nl[i, :, b, :] = noisy[i, :, b * 128 : (b + 1) * 128]
    lane_chi = iota((64, 128), 1) >> 5
    vel = [jnp.zeros((64, 128), F32)] * 2
    for chi in range(4):
        for a in range(2):
            vel[a] = jnp.where(lane_chi == chi, ve[a, pl.ds(chi, 64, stride=4), :], vel[a])
    for i in range(2):
        sigma = noise_level(time_ref[i], (16, 128))
        for p in range(2):
            for a in range(2):
                r = 2 * p + a
                part = vel[a][(i * 2 + p) * 16 : (i * 2 + p) * 16 + 16, :]
                latsend[i, r * 16 : r * 16 + 16, :] = (
                    (nl[i, r] - sigma * part) / LSCALE + LSHIFT
                ).astype(BF)

    pl.semaphore_wait(bar, 45)

    main_pos = 1 + c
    halo_j = 2 * y + zh + 2 * c - 1
    halo_pos = 3 - 3 * c
    halo_ok = (halo_j >= 0) & (halo_j <= 7)
    self_main = c == zh

    def lat_copies(h):
        here = zh == h
        main = pltpu.make_async_remote_copy(
            src_ref=latsend.at[h], dst_ref=rbuf.at[main_pos],
            send_sem=lat_s.at[2 * h], recv_sem=lat_r.at[main_pos],
            device_id={"tok": y * 2 + h, "grp": zh}, device_id_type=MESH,
        )
        halo = pltpu.make_async_remote_copy(
            src_ref=latsend.at[h], dst_ref=rbuf.at[halo_pos],
            send_sem=lat_s.at[2 * h + 1], recv_sem=lat_r.at[halo_pos],
            device_id={"tok": lax.div(halo_j, 2) * 2 + h, "grp": lax.rem(halo_j, 2)},
            device_id_type=MESH,
        )
        main_ok = jnp.logical_not(here & self_main)
        far_ok = halo_ok & jnp.logical_not(here & jnp.logical_not(self_main))
        return (main, main_ok), (halo, far_ok)

    for h in range(2):
        for copy, ok in lat_copies(h):
            pl.when(ok)(copy.start)
    self_pos = jnp.where(self_main, main_pos, halo_pos)
    rbuf[self_pos] = latsend[zh]

    @pl.when(j == 0)
    def _():
        rbuf[0] = jnp.zeros((64, 128), BF)

    @pl.when(j == 7)
    def _():
        rbuf[3] = jnp.zeros((64, 128), BF)

    for copy in loads[5:11]:
        copy.wait()

    def clear(i, carry):
        wb[pl.ds(pl.multiple_of(i * 16, 16), 16), :] = jnp.zeros((16, 8 * CH), BF)
        return carry

    lax.fori_loop(0, 32, clear, 0)
    for dy in range(3):
        for dx in range(3):
            tap = ink[dy, dx]
            for o in range(8):
                i = o + dx - 1
                row = 384 + 32 * dy if i < 0 else 384 + 32 * dy + 16 if i > 7 else dy * 128 + 16 * i
                wb[row : row + 16, o * CH : (o + 1) * CH] = tap
    rgbt = mm_nt(one_hot(iota((8, 3), 0) == iota((8, 3), 1)), rgb[...]).astype(BF)

    def wait_lat(pos, ok):
        copy = pltpu.make_async_remote_copy(
            src_ref=latsend.at[0], dst_ref=rbuf.at[pos],
            send_sem=lat_s.at[0], recv_sem=lat_r.at[pos],
            device_id={"tok": tok, "grp": 1 - c}, device_id_type=MESH,
        )
        pl.when(ok & (self_pos != pos))(copy.wait_recv)

    wait_lat(0, j > 0)
    wait_lat(1, j >= 0)
    wait_lat(2, j >= 0)
    wait_lat(3, j < 7)

    lat = rbuf[...].reshape(256, 128)
    lat32 = lat.astype(F32)
    blk = iota((256, 128), 0) & 15
    lane = iota((256, 128), 1)
    after = jnp.where((lane < 16) & (blk < 15), pltpu.roll(lat32, 255, 0), 0.0)
    before = jnp.where((lane >= 112) & (blk > 0), pltpu.roll(lat32, 1, 0), 0.0)
    edge = after + before
    side = sum(
        pltpu.roll(edge, 16 + 32 * dy, 1)[16 * dy : 16 * dy + 224] for dy in range(3)
    )
    for dy in range(3):
        lhs[:, dy * 128 : dy * 128 + 128] = lat[16 * dy : 16 * dy + 224]
    lhs[:, 384:512] = side.astype(BF)

    sum_one = jnp.zeros((8, CH), F32)
    sum_two = jnp.zeros((8, CH), F32)
    for o in range(8):
        out = mm(lhs[...], wb[:, o * CH : (o + 1) * CH]) + inb[...]
        first[:, o] = out.reshape(14, 16, CH)
        own = out[48:176].reshape(16, 8, CH)
        sum_one = sum_one + jnp.sum(own, axis=0)
        sum_two = sum_two + jnp.sum(own * own, axis=0)

    def pack(buf, rows):
        for n, row in enumerate(rows):
            row = jnp.sum(row, axis=0, keepdims=True)
            for k in range(4):
                buf[j, n * 4 + k : n * 4 + k + 1, :] = row[:, k * 128 : k * 128 + 128]

    def exchange(phase, buf):
        copies = []
        for d in range(1, 8):
            n = lax.rem(j + d, 8)
            copies.append(
                pltpu.make_async_remote_copy(
                    src_ref=buf.at[j], dst_ref=buf.at[j],
                    send_sem=ex_s.at[phase, d - 1], recv_sem=ex_r.at[phase, d - 1],
                    device_id={"tok": lax.div(n, 2) * 2 + zh, "grp": lax.rem(n, 2)},
                    device_id_type=MESH,
                )
            )
        for copy in copies:
            copy.start()
        return copies

    def collect(buf, copies):
        for copy in copies:
            copy.wait_recv()
        total = buf[0]
        for k in range(1, 8):
            total = total + buf[k]
        return total

    def as_row(tile, start):
        rowbuf[...] = tile
        return jnp.concatenate([rowbuf[start + k : start + k + 1, :] for k in range(4)], axis=1)

    pack(p1, (sum_one, sum_two))
    ex1 = exchange(0, p1)

    def flip(k, carry):
        start = pl.multiple_of(k * 128, 128)
        modt[pl.ds(start, 128), :] = mod[:, pl.ds(start, 128)].astype(F32).T.astype(BF)
        return carry

    lax.fori_loop(0, 19, flip, 0)
    half = D // 2
    other_start = pl.multiple_of((1 - c) * half, 64)
    mod_copy = pltpu.make_async_remote_copy(
        src_ref=modt.at[pl.ds(other_start, half), :], dst_ref=modp,
        send_sem=mod_s, recv_sem=mod_r,
        device_id={"grp": 1 - c}, device_id_type=MESH,
    )
    mod_copy.start()

    stats = group_total(collect(p1, ex1)) / GROUP_N
    mu = as_row(stats, 0)
    rstd = lax.rsqrt(as_row(stats, 4) - mu * mu + EPS)
    coef_a = rstd * gain[...] * 0.5
    coef_b = (nbias[...] - mu * rstd * gain[...]) * 0.5

    blk16 = iota((16, CH), 0)

    def put_row(buf, r, value):
        buf[r, 1:9] = value.astype(BF)
        buf[r, 0] = jnp.where(blk16 > 0, pltpu.roll(value[7], 1, 0), 0.0).astype(BF)
        buf[r, 9] = jnp.where(blk16 < 15, pltpu.roll(value[0], 15, 0), 0.0).astype(BF)

    def inside(row):
        return ((row >= 0) & (row < 64)).astype(F32)

    def act_row(r, carry):
        half_u = first[r] * coef_a + coef_b
        value = half_u * (1.0 + jnp.tanh(half_u)) * inside(8 * j - 3 + r)
        put_row(act, r, value)
        return carry

    lax.fori_loop(0, 14, act_row, 0)

    loads[11].wait()

    def decode(pieces):
        total = None
        for dy in range(3):
            for dx in range(3):
                part = [act[pl.ds(r + dy, n), dx : dx + 8].reshape(n * 128, CH) for r, n in pieces]
                part = part[0] if len(part) == 1 else jnp.concatenate(part, axis=0)
                term = mm(part, midk[dy, dx])
                total = term if total is None else total + term
        half_u = (total + midb[...]) * 0.5
        tanh = jnp.tanh(half_u)
        grad = 0.5 * ((1.0 + tanh) + half_u * (1.0 - tanh * tanh))
        return half_u * (1.0 + tanh), grad

    def own_decode(i, total):
        r = 2 + 4 * i
        value, grad = decode([(r, 4)])
        slope[pl.ds(r, 4)] = grad.reshape(4, 8, 16, CH)
        pixel = mm_nt(rgbt, value.astype(BF))
        for colour in range(3):
            for row in range(4):
                pixg[zh, j, pl.ds(colour * 8 + 4 * i + row, 1), :] = (
                    pixel[colour : colour + 1, row * 128 : row * 128 + 128]
                )
        return total + jnp.sum(value.reshape(64, 8, CH), axis=0)

    pooled_sum = lax.fori_loop(0, 2, own_decode, jnp.zeros((8, CH), F32))
    pack(p2, (pooled_sum,))
    ex2 = exchange(1, p2)

    pix_copies = []
    for d in range(1, 16):
        n = lax.rem(tok * 2 + c + d, 16)
        pix_copies.append(
            pltpu.make_async_remote_copy(
                src_ref=pixg.at[zh, j], dst_ref=pixg.at[zh, j],
                send_sem=pix_s.at[d - 1], recv_sem=pix_r.at[d - 1],
                device_id={"tok": lax.div(n, 2), "grp": lax.rem(n, 2)}, device_id_type=MESH,
            )
        )
    for copy in pix_copies:
        copy.start()

    _, grad = decode([(0, 2), (10, 2)])
    slope[0:2] = grad[:256].reshape(2, 8, 16, CH)
    slope[10:12] = grad[256:].reshape(2, 8, 16, CH)

    loads[12].wait()
    loads[13].wait()
    pooled = (as_row(collect(p2, ex2), 0) / CELLS).astype(BF)
    feature = mm(jnp.broadcast_to(pooled, (8, CH)), clip[...])
    target = text[pl.ds(zh, 1), :]
    norm_f = jnp.sqrt(jnp.sum(feature * feature, axis=-1, keepdims=True) + EPS)
    norm_t = jnp.sqrt(jnp.sum(target * target, axis=-1, keepdims=True) + EPS)
    reward = jnp.sum(feature * target, axis=-1, keepdims=True) / (norm_f * norm_t)
    grad_feature = (
        REWARD_W * (target / (norm_f * norm_t) - reward * feature / (norm_f * norm_f))
    ).astype(BF)
    grad_act = mm_nt(grad_feature, clip[...])[0:1, :]
    rewb[zh] = jnp.broadcast_to(reward, (8, 128))
    rew_copy = pltpu.make_async_remote_copy(
        src_ref=rewb.at[zh], dst_ref=rewb.at[zh], send_sem=rew_s, recv_sem=rew_r,
        device_id={"tok": y * 2 + 1 - zh}, device_id_type=MESH,
    )
    rew_copy.start()

    def grad_row(r, carry):
        put_row(gsec, r, slope[r] * grad_act * inside(8 * j - 2 + r))
        return carry

    lax.fori_loop(0, 12, grad_row, 0)

    xh_b = mu * rstd

    def back(pieces):
        total = None
        for dy in range(3):
            for dx in range(3):
                part = [
                    gsec[pl.ds(r + 2 - dy, n), 2 - dx : 10 - dx].reshape(n * 128, CH)
                    for r, n in pieces
                ]
                part = part[0] if len(part) == 1 else jnp.concatenate(part, axis=0)
                term = mm_nt(part, midk[dy, dx])
                total = term if total is None else total + term
        value = [first[pl.ds(r + 2, n)].reshape(n * 128, CH) for r, n in pieces]
        value = value[0] if len(value) == 1 else jnp.concatenate(value, axis=0)
        half_u = value * coef_a + coef_b
        tanh = jnp.tanh(half_u)
        grad = 0.5 * ((1.0 + tanh) + half_u * (1.0 - tanh * tanh))
        return total * (grad * gain[...]), value * rstd - xh_b

    def own_back(i, carry):
        r = 1 + 4 * i
        w, xhat = back([(r, 4)])
        wgr[pl.ds(r, 4)] = w.reshape(4, 8, 16, CH)
        return (
            carry[0] + jnp.sum(w.reshape(64, 8, CH), axis=0),
            carry[1] + jnp.sum((w * xhat).reshape(64, 8, CH), axis=0),
        )

    zero = jnp.zeros((8, CH), F32)
    sums = lax.fori_loop(0, 2, own_back, (zero, zero))
    pack(p3, sums)
    ex3 = exchange(2, p3)
    w, _ = back([(0, 1), (9, 1)])
    wgr[0:1] = w[:128].reshape(1, 8, 16, CH)
    wgr[9:10] = w[128:].reshape(1, 8, 16, CH)

    stats = group_total(collect(p3, ex3)) / GROUP_N
    mean_w = as_row(stats, 0)
    mean_x = as_row(stats, 4)
    coef_f = -rstd * rstd * mean_x
    coef_0 = (xh_b * mean_x - mean_w) * rstd

    def first_row(r, carry):
        value = wgr[r] * rstd + first[r + 2] * coef_f + coef_0
        value = (value * inside(8 * j - 1 + r)).astype(BF)
        start = pl.multiple_of(r * 16, 16)
        for o in range(8):
            gfc[pl.ds(start, 16), o * CH : (o + 1) * CH] = value[o]
        return carry

    lax.fori_loop(0, 10, first_row, 0)
    back_y = mm_nt(gfc[...], wb[...])
    grad_lat = jnp.zeros((128, 128), F32)
    edge = jnp.zeros((128, 128), F32)
    lane = iota((128, 128), 1)
    blk = iota((128, 128), 0) & 15
    for dy in range(3):
        start = (2 - dy) * 16
        grad_lat = grad_lat + back_y[start : start + 128, dy * 128 : dy * 128 + 128]
        part = back_y[start : start + 128, 384:512]
        part = jnp.where((lane >> 5) == dy, part, 0.0)
        edge = edge + pltpu.roll(part, (112 - 32 * dy) % 128, 1)
    grad_lat = grad_lat + jnp.where((lane >= 112) & (blk < 15), pltpu.roll(edge, 127, 0), 0.0)
    grad_lat = grad_lat + jnp.where((lane < 16) & (blk > 0), pltpu.roll(edge, 1, 0), 0.0)
    sigma = noise_level(time_ref[zh], (128, 128))
    gvsend[...] = (-sigma * (grad_lat / LSCALE)).astype(BF).reshape(2, 64, 128)

    def gv_copy(e):
        copy = pltpu.make_async_remote_copy(
            src_ref=gvsend, dst_ref=gvr.at[zh],
            send_sem=gv_s.at[e], recv_sem=gv_r.at[zh],
            device_id={"tok": y * 2 + c, "grp": e}, device_id_type=MESH,
        )
        return copy, jnp.logical_not((c == zh) & (c == e))

    for e in range(2):
        copy, ok = gv_copy(e)
        pl.when(ok)(copy.start)

    @pl.when(c == zh)
    def _():
        gvr[zh] = gvsend[...]

    for h in range(2):
        copy = pltpu.make_async_remote_copy(
            src_ref=gvsend, dst_ref=gvr.at[h],
            send_sem=gv_s.at[0], recv_sem=gv_r.at[h],
            device_id={"tok": y * 2 + c, "grp": 0}, device_id_type=MESH,
        )
        pl.when(jnp.logical_not((c == zh) & (zh == h)))(copy.wait_recv)

    def tokens(e):
        for a in range(2):
            rows = [
                gvr[i, e, (2 * p + a) * 16 : (2 * p + a) * 16 + 16, :]
                for i in range(2) for p in range(2)
            ]
            full = jnp.concatenate(rows, axis=0).astype(F32)
            for chi in range(4):
                ve[a, pl.ds(chi, 64, stride=4), :] = jnp.where(lane_chi == chi, full, 0.0)
        return jnp.concatenate([ve[0], ve[1]], axis=1).astype(BF)

    j_r, k_c = iota((256, 256), 0), iota((256, 256), 1)
    target_lane = j_r & 63
    keep = ((target_lane >> 5) == (k_c >> 7)) & ((target_lane & 31) == (k_c & 31))
    quad = one_hot(keep & ((j_r < 64) | (j_r >= 192)))
    mine = tokens(c)
    mine_gv = mm_nt(mine, quad).astype(BF)
    theirs_gv = mm_nt(tokens(1 - c), quad).astype(BF)
    mod_copy.wait_recv()
    own_start = c * half
    term = mm(modt[pl.ds(pl.multiple_of(own_start, 64), 608), :], mine_gv[:, :128])
    term = term + mm(modt[pl.ds(pl.multiple_of(own_start + 608, 32), 608), :], mine_gv[:, 128:])
    term = term + mm(modp[0:608, :], theirs_gv[:, :128])
    term = term + mm(modp[608:1216, :], theirs_gv[:, 128:])
    wt[...] = term * (1.0 / 2048.0)
    for k in range(16):
        s1send[k, 0:32, :] = wt[38 * k : 38 * k + 32, :].astype(BF)
        tail = jnp.concatenate([wt[38 * k + 32 : 38 * k + 38, :], jnp.zeros((10, 128), F32)], axis=0)
        s1send[k, 32:48, :] = tail.astype(BF)
    me_xy = x * 4 + y
    s1 = []
    for d in range(1, 16):
        n = lax.rem(me_xy + d, 16)
        s1.append(
            pltpu.make_async_remote_copy(
                src_ref=s1send.at[n], dst_ref=s1recv.at[me_xy],
                send_sem=s1_s.at[d - 1], recv_sem=s1_r.at[d - 1],
                device_id={"batch": zl * 4 + lax.div(n, 4), "tok": lax.rem(n, 4) * 2 + zh},
                device_id_type=MESH,
            )
        )
    for copy in s1:
        copy.start()
    s1recv[me_xy] = s1send[me_xy]

    own_tokens[...] = mine

    def hidden_rows(i, carry):
        img, start = lax.div(i, 4), pl.multiple_of(lax.rem(i, 4) * 32, 32)
        flat = pl.multiple_of(i * 32, 32)
        grad_mod = mm_nt(own_tokens[pl.ds(flat, 32), :], wrep[...])
        inv = stat_i[pl.ds(flat, 32), :]
        normal = (hid[img, pl.ds(start, 32), :].astype(F32) - stat_m[pl.ds(flat, 32), :]) * inv
        e = grad_mod * (1.0 + scalev[pl.ds(img, 1), :])
        mean_e = jnp.sum(e, axis=-1, keepdims=True) / D
        mean_n = jnp.sum(e * normal, axis=-1, keepdims=True) / D
        hgv[img, pl.ds(start, 32), :] = (inv * (e - mean_e - normal * mean_n)).astype(BF)
        return carry

    lax.fori_loop(0, 8, hidden_rows, 0)
    hg_copy = pltpu.make_async_copy(hgv, hg_h, out_sem)
    hg_copy.start()

    for copy in s1:
        copy.wait_recv()
    total = s1recv[0].astype(F32)
    for k in range(1, 16):
        total = total + s1recv[k].astype(F32)
    wt[0:48, :] = total
    for z in range(2):
        s2send[z] = wt[19 * z : 19 * z + 24, :]
    me_z = zl * 2 + zh

    def line_copy(n):
        dest_zl, dest_zh, dest_c = 2 * c + n // 4, (n // 2) % 2, n % 2
        copy = pltpu.make_async_remote_copy(
            src_ref=s2send.at[dest_zh], dst_ref=s2recv.at[me_z],
            send_sem=s2_s.at[n], recv_sem=s2_r.at[me_z],
            device_id={"batch": dest_zl * 4 + x, "tok": y * 2 + dest_zh, "grp": dest_c},
            device_id_type=MESH,
        )
        return copy, jnp.logical_not((dest_zl == zl) & (dest_zh == zh) & (dest_c == c))

    for n in range(8):
        copy, ok = line_copy(n)
        pl.when(ok)(copy.start)
    self_line = lax.div(zl, 2) == c

    @pl.when(self_line)
    def _():
        s2recv[me_z] = s2send[zh]

    for copy in pix_copies:
        copy.wait_recv()
    l384, k384 = iota((384, 384), 0), iota((384, 384), 1)
    cell = l384 & 127
    place = jnp.where(k384 == ((cell & 15) * 8 + (cell >> 4)) * 3 + (l384 >> 7), 1.0, 0.0)
    for i in range(2):
        slab = map_ref[i, 0]
        block = pixg[i, slab >> 1]
        odd = jnp.full((24, 128), slab & 1, jnp.int32) == 1
        block = jnp.where(odd, pltpu.roll(block, 20, 0), block)
        wide = jnp.concatenate([block[0:8], block[8:16], block[16:24]], axis=1)
        moved = lax.dot_general(
            wide, place, (((1,), (0,)), ((), ())),
            precision=lax.Precision.HIGHEST, preferred_element_type=F32,
        )
        pix_out[i, 0] = moved[0:4]

    rew_copy.wait_recv()
    lane = iota((1, 128), 1)
    rew_out[...] = jnp.where(lane == 0, rewb[0, 0:1, :], rewb[1, 0:1, :])[:, 0:2]

    for n in range(8):
        copy = pltpu.make_async_remote_copy(
            src_ref=s2send.at[0], dst_ref=s2recv.at[n],
            send_sem=s2_s.at[0], recv_sem=s2_r.at[n],
            device_id={"grp": 1 - c}, device_id_type=MESH,
        )
        pl.when(jnp.logical_not(self_line & (me_z == n)))(copy.wait_recv)
    total = s2recv[0]
    for k in range(1, 8):
        total = total + s2recv[k]
    odd = jnp.full((24, 128), lax.rem(zl, 2), jnp.int32) == 1
    total = jnp.where(odd, pltpu.roll(total, 64, 1), total)
    wg_ref[...] = total[0:19, 0:64]

    for h in range(2):
        for copy, ok in lat_copies(h):
            pl.when(ok)(copy.wait_send)
    for copy in ex1 + ex2 + ex3 + pix_copies + s1 + [rew_copy, mod_copy]:
        copy.wait_send()
    for e in range(2):
        copy, ok = gv_copy(e)
        pl.when(ok)(copy.wait_send)
    for n in range(8):
        copy, ok = line_copy(n)
        pl.when(ok)(copy.wait_send)
    hg_copy.wait()


def local(
    hidden, shift, scale, out_weight, noisy_latent, timestep, in_kernel, in_bias,
    norm_gain, norm_bias, mid_kernel, mid_bias, rgb_weight, clip_weight, text_embed, slab_map,
):
    any_spec = pl.BlockSpec(memory_space=pl.ANY)
    smem = pl.BlockSpec(memory_space=pltpu.SMEM)
    vmem = pl.BlockSpec(memory_space=pltpu.VMEM)
    dma = pltpu.SemaphoreType.DMA

    def v(dtype, *shape):
        return pltpu.VMEM(shape, dtype)

    hg, wg, reward, pixels = pl.pallas_call(
        kernel,
        out_shape=(
            jax.ShapeDtypeStruct((2, 128, D), BF),
            jax.ShapeDtypeStruct((19, 64), F32),
            jax.ShapeDtypeStruct((1, 2), F32),
            jax.ShapeDtypeStruct((2, 1, 4, 384), F32),
        ),
        in_specs=[smem, smem] + [any_spec] * 14,
        out_specs=(any_spec, vmem, vmem, vmem),
        scratch_shapes=[
            v(BF, 2, 128, D), v(F32, 2, D), v(F32, 2, D), v(BF, D, 64), v(F32, 2, 4, 2048),
            v(BF, 3, 3, 16, CH), v(F32, 1, CH), v(F32, 1, CH), v(F32, 1, CH),
            v(BF, 3, 3, CH, CH), v(F32, 1, CH), v(BF, CH, 3), v(BF, CH, EMB), v(F32, 2, EMB),
            v(F32, 256, 1), v(F32, 256, 1), v(BF, 256, D), v(BF, D, 256), v(BF, D // 2, 256),
            v(BF, D, 256), v(F32, 2, 256, 128), v(F32, 2, 4, 16, 128), v(BF, 2, 64, 128),
            v(BF, 4, 64, 128), v(BF, 224, 512), v(BF, 512, 8 * CH),
            v(F32, 14, 8, 16, CH), v(BF, 14, 10, 16, CH), v(F32, 12, 8, 16, CH),
            v(BF, 12, 10, 16, CH), v(F32, 10, 8, 16, CH), v(BF, 160, 8 * CH), v(F32, 8, 128),
            v(F32, 8, 8, 128), v(F32, 8, 8, 128), v(F32, 8, 8, 128), v(F32, 2, 8, 128),
            v(F32, 2, 8, 24, 128), v(BF, 2, 64, 128), v(BF, 2, 2, 64, 128), v(F32, 608, 128),
            v(BF, 16, 48, 128), v(BF, 16, 48, 128), v(F32, 2, 24, 128), v(F32, 8, 24, 128),
            v(BF, 2, 128, D), v(BF, 256, 256),
            dma((14,)), dma((4,)), dma((4,)), dma((3, 7)), dma((3, 7)), dma((15,)), dma((15,)),
            dma, dma, dma, dma, dma((2,)), dma((2,)), dma((15,)), dma((15,)), dma((8,)), dma((8,)),
            dma,
        ],
        compiler_params=pltpu.CompilerParams(
            collective_id=0, has_side_effects=True, vmem_limit_bytes=58 * 2**20
        ),
    )(
        timestep, slab_map, hidden, shift, scale, out_weight, noisy_latent, in_kernel,
        in_bias.reshape(1, CH), norm_gain.reshape(1, CH), norm_bias.reshape(1, CH),
        mid_kernel, mid_bias.reshape(1, CH), rgb_weight, clip_weight, text_embed,
    )
    return hg, wg, reward.reshape(2), pixels


def solution(mesh):
    rows = ("tok", "grp")
    return jax.shard_map(
        local,
        mesh=mesh,
        in_specs=(
            P("batch", rows, None), P("batch", None), P("batch", None), P(),
            P("batch", rows, None), P("batch"), P(), P(), P(), P(), P(), P(), P(), P(),
            P("batch", None), P("batch", rows),
        ),
        out_specs=(
            P("batch", rows, None), P(("batch", "tok"), None), P("batch"),
            P("batch", rows, None, None),
        ),
        check_vma=False,
    )
```

```python
import jax
import jax.numpy as jnp
from jax import lax
from jax.experimental import pallas as pl
from jax.experimental.pallas import tpu as pltpu
from jax.sharding import PartitionSpec as P

D = 2432
CH = 512
EMB = 1024
GROUP_N = 131072.0
CELLS = 8192.0
EPS = 1e-6
LSCALE = 1.5305
LSHIFT = 0.0609
REWARD_W = 16.0
BF = jnp.bfloat16
F32 = jnp.float32
MESH = pl.DeviceIdType.MESH

NT = (((1,), (1,)), ((), ()))


def mm(a, b):
    return jnp.dot(a, b, preferred_element_type=F32)


def mm_nt(a, b):
    return lax.dot_general(a, b, NT, preferred_element_type=F32)


def iota(shape, dim):
    return lax.broadcasted_iota(jnp.int32, shape, dim)


def one_hot(cond):
    return jnp.where(cond, 1.0, 0.0).astype(BF)


def noise_level(step, shape):
    fraction = (jnp.full(shape, step, jnp.int32).astype(F32) + 1.0) / 1000.0
    return 3.0 * fraction / (1.0 + 2.0 * fraction)


def group_total(tile):
    lane = iota(tile.shape, 1)
    for step in (1, 2, 4, 8):
        tile = tile + jnp.where(
            (lane & step) != 0, pltpu.roll(tile, step, 1), pltpu.roll(tile, 128 - step, 1)
        )
    return tile


def kernel(
    time_ref, map_ref,
    hidden_h, shift_h, scale_h, outw_h, noisy_h, ink_h, inb_h, gain_h, nbias_h,
    midk_h, midb_h, rgb_h, clip_h, text_h,
    hgv, wg_ref, rew_out, pix_out,
    hid, shiftv, scalev, outw, noisy, ink, inb, gain, nbias, midk, midb, rgb, clip, text,
    stat_m, stat_i, mod, modt, modp, wrep, ve, nl, latsend, rbuf, lhs, wb,
    first, act, slope, gsec, wgr, gfc, rowbuf,
    p1, p2, p3, rewb, pixg, gvx, gvr, wt, s1send, s1recv, s2send, s2recv, own_tokens,
    load_sem, lat_s, lat_r, ex_s, ex_r, pix_s, pix_r, rew_s, rew_r, mod_s, mod_r,
    gx_s, gx_r, gv_s, gv_r, s1_s, s1_r, s2_s, s2_r,
):
    bt = lax.axis_index("batch")
    tok = lax.axis_index("tok")
    c = lax.axis_index("grp")
    y, zh = lax.div(tok, 2), lax.rem(tok, 2)
    zl, x = lax.div(bt, 4), lax.rem(bt, 4)
    j = 2 * y + c

    pairs = [
        (outw_h, outw), (scale_h, scalev), (shift_h, shiftv), (hidden_h, hid),
        (noisy_h, noisy), (ink_h, ink), (inb_h, inb), (gain_h, gain), (nbias_h, nbias),
        (midb_h, midb), (rgb_h, rgb), (midk_h, midk), (clip_h, clip), (text_h, text),
    ]
    loads = [
        pltpu.make_async_copy(src, dst, load_sem.at[i]) for i, (src, dst) in enumerate(pairs)
    ]
    for copy in loads:
        copy.start()

    bar = pltpu.get_barrier_semaphore()
    for d in range(1, 16):
        n = lax.rem(tok * 2 + c + d, 16)
        pl.semaphore_signal(
            bar, inc=1, device_id={"tok": lax.div(n, 2), "grp": lax.rem(n, 2)}, device_id_type=MESH
        )
        n = lax.rem(x * 4 + y + d, 16)
        pl.semaphore_signal(
            bar, inc=1,
            device_id={"batch": zl * 4 + lax.div(n, 4), "tok": lax.rem(n, 4) * 2 + zh},
            device_id_type=MESH,
        )
        n = lax.rem((zl * 2 + zh) * 2 + c + d, 16)
        pl.semaphore_signal(
            bar, inc=1,
            device_id={
                "batch": lax.div(n, 4) * 4 + x,
                "tok": y * 2 + lax.rem(lax.div(n, 2), 2),
                "grp": lax.rem(n, 2),
            },
            device_id_type=MESH,
        )

    loads[0].wait()
    j256, k64 = iota((256, 64), 0), iota((256, 64), 1)
    spread = one_hot(((k64 >> 5) == (j256 >> 7)) & ((k64 & 31) == (j256 & 31)))
    wrep[...] = mm(spread, outw[...]).astype(BF)

    for copy in loads[1:4]:
        copy.wait()

    def norm_rows(i, carry):
        img, start = lax.div(i, 4), pl.multiple_of(lax.rem(i, 4) * 32, 32)
        flat = pl.multiple_of(i * 32, 32)
        values = hid[img, pl.ds(start, 32), :].astype(F32)
        mean = jnp.sum(values, axis=-1, keepdims=True) / D
        centered = values - mean
        inv = lax.rsqrt(jnp.sum(centered * centered, axis=-1, keepdims=True) / D + EPS)
        stat_m[pl.ds(flat, 32), :] = mean
        stat_i[pl.ds(flat, 32), :] = inv
        gain_row = 1.0 + scalev[pl.ds(img, 1), :]
        mod[pl.ds(flat, 32), :] = (
            centered * inv * gain_row + shiftv[pl.ds(img, 1), :]
        ).astype(BF)
        return carry

    lax.fori_loop(0, 8, norm_rows, 0)
    velocity = mm_nt(mod[...], wrep[...])
    for a in range(2):
        ve[a] = velocity[:, a * 128 : a * 128 + 128]

    loads[4].wait()
    for i in range(2):
        for b in range(16):
            nl[i, :, b, :] = noisy[i, :, b * 128 : (b + 1) * 128]
    lane_chi = iota((64, 128), 1) >> 5
    vel = [jnp.zeros((64, 128), F32)] * 2
    for chi in range(4):
        for a in range(2):
            vel[a] = jnp.where(lane_chi == chi, ve[a, pl.ds(chi, 64, stride=4), :], vel[a])
    for i in range(2):
        sigma = noise_level(time_ref[i], (16, 128))
        for p in range(2):
            for a in range(2):
                r = 2 * p + a
                part = vel[a][(i * 2 + p) * 16 : (i * 2 + p) * 16 + 16, :]
                latsend[i, r * 16 : r * 16 + 16, :] = (
                    (nl[i, r] - sigma * part) / LSCALE + LSHIFT
                ).astype(BF)

    pl.semaphore_wait(bar, 45)

    main_pos = 1 + c
    halo_j = 2 * y + zh + 2 * c - 1
    halo_pos = 3 - 3 * c
    halo_ok = (halo_j >= 0) & (halo_j <= 7)
    self_main = c == zh

    def lat_copies(h):
        here = zh == h
        main = pltpu.make_async_remote_copy(
            src_ref=latsend.at[h], dst_ref=rbuf.at[main_pos],
            send_sem=lat_s.at[2 * h], recv_sem=lat_r.at[main_pos],
            device_id={"tok": y * 2 + h, "grp": zh}, device_id_type=MESH,
        )
        halo = pltpu.make_async_remote_copy(
            src_ref=latsend.at[h], dst_ref=rbuf.at[halo_pos],
            send_sem=lat_s.at[2 * h + 1], recv_sem=lat_r.at[halo_pos],
            device_id={"tok": lax.div(halo_j, 2) * 2 + h, "grp": lax.rem(halo_j, 2)},
            device_id_type=MESH,
        )
        main_ok = jnp.logical_not(here & self_main)
        far_ok = halo_ok & jnp.logical_not(here & jnp.logical_not(self_main))
        return (main, main_ok), (halo, far_ok)

    for h in range(2):
        for copy, ok in lat_copies(h):
            pl.when(ok)(copy.start)
    self_pos = jnp.where(self_main, main_pos, halo_pos)
    rbuf[self_pos] = latsend[zh]

    @pl.when(j == 0)
    def _():
        rbuf[0] = jnp.zeros((64, 128), BF)

    @pl.when(j == 7)
    def _():
        rbuf[3] = jnp.zeros((64, 128), BF)

    for copy in loads[5:11]:
        copy.wait()

    def clear(i, carry):
        wb[pl.ds(pl.multiple_of(i * 16, 16), 16), :] = jnp.zeros((16, 8 * CH), BF)
        return carry

    lax.fori_loop(0, 32, clear, 0)
    for dy in range(3):
        for dx in range(3):
            tap = ink[dy, dx]
            for o in range(8):
                i = o + dx - 1
                row = 384 + 32 * dy if i < 0 else 384 + 32 * dy + 16 if i > 7 else dy * 128 + 16 * i
                wb[row : row + 16, o * CH : (o + 1) * CH] = tap
    rgbt = mm(one_hot(iota((8, 3), 0) == iota((8, 3), 1)), rgb[...]).astype(BF)

    def wait_lat(pos, ok):
        copy = pltpu.make_async_remote_copy(
            src_ref=latsend.at[0], dst_ref=rbuf.at[pos],
            send_sem=lat_s.at[0], recv_sem=lat_r.at[pos],
            device_id={"tok": tok, "grp": 1 - c}, device_id_type=MESH,
        )
        pl.when(ok & (self_pos != pos))(copy.wait_recv)

    wait_lat(0, j > 0)
    wait_lat(1, j >= 0)
    wait_lat(2, j >= 0)
    wait_lat(3, j < 7)

    lat = rbuf[...].reshape(256, 128)
    lat32 = lat.astype(F32)
    blk = iota((256, 128), 0) & 15
    lane = iota((256, 128), 1)
    after = jnp.where((lane < 16) & (blk < 15), pltpu.roll(lat32, 255, 0), 0.0)
    before = jnp.where((lane >= 112) & (blk > 0), pltpu.roll(lat32, 1, 0), 0.0)
    edge = after + before
    side = sum(
        pltpu.roll(edge, 16 + 32 * dy, 1)[16 * dy : 16 * dy + 224] for dy in range(3)
    )
    for dy in range(3):
        lhs[:, dy * 128 : dy * 128 + 128] = lat[16 * dy : 16 * dy + 224]
    lhs[:, 384:512] = side.astype(BF)

    sum_one = jnp.zeros((8, CH), F32)
    sum_two = jnp.zeros((8, CH), F32)
    for o in range(8):
        out = mm(lhs[...], wb[:, o * CH : (o + 1) * CH]) + inb[...]
        first[:, o] = out.reshape(14, 16, CH)
        own = out[48:176].reshape(16, 8, CH)
        sum_one = sum_one + jnp.sum(own, axis=0)
        sum_two = sum_two + jnp.sum(own * own, axis=0)

    def pack(buf, rows):
        for n, row in enumerate(rows):
            row = jnp.sum(row, axis=0, keepdims=True)
            for k in range(4):
                buf[j, n * 4 + k : n * 4 + k + 1, :] = row[:, k * 128 : k * 128 + 128]

    def exchange(phase, buf):
        copies = []
        for d in range(1, 8):
            n = lax.rem(j + d, 8)
            copies.append(
                pltpu.make_async_remote_copy(
                    src_ref=buf.at[j], dst_ref=buf.at[j],
                    send_sem=ex_s.at[phase, d - 1], recv_sem=ex_r.at[phase, d - 1],
                    device_id={"tok": lax.div(n, 2) * 2 + zh, "grp": lax.rem(n, 2)},
                    device_id_type=MESH,
                )
            )
        for copy in copies:
            copy.start()
        return copies

    def collect(buf, copies):
        for copy in copies:
            copy.wait_recv()
        total = buf[0]
        for k in range(1, 8):
            total = total + buf[k]
        return total

    def as_row(tile, start):
        rowbuf[...] = tile
        return jnp.concatenate([rowbuf[start + k : start + k + 1, :] for k in range(4)], axis=1)

    pack(p1, (sum_one, sum_two))
    ex1 = exchange(0, p1)

    def flip(k, carry):
        start = pl.multiple_of(k * 128, 128)
        for h in range(2):
            block = mod[h * 128 : h * 128 + 128, pl.ds(start, 128)]
            modt[h, pl.ds(start, 128), :] = block.astype(F32).T.astype(BF)
        return carry

    lax.fori_loop(0, 19, flip, 0)
    half = D // 2
    place4 = zh * 2 + c
    mod_lane = pl.ds(pl.multiple_of(place4 * 128, 128), 128)
    mod_copies = []
    for d in range(1, 4):
        n = lax.rem(place4 + d, 4)
        h, core = lax.div(n, 2), lax.rem(n, 2)
        mod_copies.append(
            pltpu.make_async_remote_copy(
                src_ref=modt.at[h, pl.ds(pl.multiple_of(core * half, 64), half), :],
                dst_ref=modp.at[:, mod_lane],
                send_sem=mod_s.at[d - 1], recv_sem=mod_r.at[d - 1],
                device_id={"tok": y * 2 + h, "grp": core}, device_id_type=MESH,
            )
        )
    for copy in mod_copies:
        copy.start()
    modp[:, mod_lane] = modt[zh, pl.ds(pl.multiple_of(c * half, 64), half), :]

    stats = group_total(collect(p1, ex1)) / GROUP_N
    mu = as_row(stats, 0)
    rstd = lax.rsqrt(as_row(stats, 4) - mu * mu + EPS)
    coef_a = rstd * gain[...] * 0.5
    coef_b = (nbias[...] - mu * rstd * gain[...]) * 0.5

    blk16 = iota((16, CH), 0)

    def put_row(buf, r, value):
        buf[r, 1:9] = value.astype(BF)
        buf[r, 0] = jnp.where(blk16 > 0, pltpu.roll(value[7], 1, 0), 0.0).astype(BF)
        buf[r, 9] = jnp.where(blk16 < 15, pltpu.roll(value[0], 15, 0), 0.0).astype(BF)

    def inside(row):
        return ((row >= 0) & (row < 64)).astype(F32)

    def act_row(r, carry):
        half_u = first[r] * coef_a + coef_b
        value = half_u * (1.0 + jnp.tanh(half_u)) * inside(8 * j - 3 + r)
        put_row(act, r, value)
        return carry

    lax.fori_loop(0, 14, act_row, 0)

    loads[11].wait()

    def decode(pieces):
        total = None
        for dy in range(3):
            for dx in range(3):
                part = [act[r + dy : r + dy + n, dx : dx + 8].reshape(n * 128, CH) for r, n in pieces]
                part = part[0] if len(part) == 1 else jnp.concatenate(part, axis=0)
                term = mm(part, midk[dy, dx])
                total = term if total is None else total + term
        half_u = (total + midb[...]) * 0.5
        tanh = jnp.tanh(half_u)
        grad = 0.5 * ((1.0 + tanh) + half_u * (1.0 - tanh * tanh))
        return half_u * (1.0 + tanh), grad

    pooled_sum = jnp.zeros((8, CH), F32)
    for i in range(4):
        r = 2 + 2 * i
        value, grad = decode([(r, 2)])
        slope[r : r + 2] = grad.reshape(2, 8, 16, CH)
        pixel = mm_nt(rgbt, value.astype(BF))
        for colour in range(3):
            for row in range(2):
                at = colour * 8 + 2 * i + row
                pixg[zh, j, at : at + 1, :] = pixel[colour : colour + 1, row * 128 : row * 128 + 128]
        pooled_sum = pooled_sum + jnp.sum(value.reshape(32, 8, CH), axis=0)

    pack(p2, (pooled_sum,))
    ex2 = exchange(1, p2)

    pix_copies = []
    for d in range(1, 16):
        n = lax.rem(tok * 2 + c + d, 16)
        pix_copies.append(
            pltpu.make_async_remote_copy(
                src_ref=pixg.at[zh, j], dst_ref=pixg.at[zh, j],
                send_sem=pix_s.at[d - 1], recv_sem=pix_r.at[d - 1],
                device_id={"tok": lax.div(n, 2), "grp": lax.rem(n, 2)}, device_id_type=MESH,
            )
        )
    for copy in pix_copies:
        copy.start()

    _, grad = decode([(0, 2), (10, 2)])
    slope[0:2] = grad[:256].reshape(2, 8, 16, CH)
    slope[10:12] = grad[256:].reshape(2, 8, 16, CH)

    loads[12].wait()
    loads[13].wait()
    pooled = (as_row(collect(p2, ex2), 0) / CELLS).astype(BF)
    feature = mm(jnp.broadcast_to(pooled, (8, CH)), clip[...])
    target = text[pl.ds(zh, 1), :]
    norm_f = jnp.sqrt(jnp.sum(feature * feature, axis=-1, keepdims=True) + EPS)
    norm_t = jnp.sqrt(jnp.sum(target * target, axis=-1, keepdims=True) + EPS)
    reward = jnp.sum(feature * target, axis=-1, keepdims=True) / (norm_f * norm_t)
    grad_feature = (
        REWARD_W * (target / (norm_f * norm_t) - reward * feature / (norm_f * norm_f))
    ).astype(BF)
    grad_act = mm_nt(grad_feature, clip[...])[0:1, :]
    rewb[zh] = jnp.broadcast_to(reward, (8, 128))
    rew_copy = pltpu.make_async_remote_copy(
        src_ref=rewb.at[zh], dst_ref=rewb.at[zh], send_sem=rew_s, recv_sem=rew_r,
        device_id={"tok": y * 2 + 1 - zh}, device_id_type=MESH,
    )
    rew_copy.start()

    def grad_row(r, carry):
        put_row(gsec, r, slope[r] * grad_act * inside(8 * j - 2 + r))
        return carry

    lax.fori_loop(0, 12, grad_row, 0)

    xh_b = mu * rstd

    def back(pieces):
        total = None
        for dy in range(3):
            for dx in range(3):
                part = [
                    gsec[r + 2 - dy : r + 2 - dy + n, 2 - dx : 10 - dx].reshape(n * 128, CH)
                    for r, n in pieces
                ]
                part = part[0] if len(part) == 1 else jnp.concatenate(part, axis=0)
                term = mm_nt(part, midk[dy, dx])
                total = term if total is None else total + term
        value = [first[r + 2 : r + 2 + n].reshape(n * 128, CH) for r, n in pieces]
        value = value[0] if len(value) == 1 else jnp.concatenate(value, axis=0)
        half_u = value * coef_a + coef_b
        tanh = jnp.tanh(half_u)
        grad = 0.5 * ((1.0 + tanh) + half_u * (1.0 - tanh * tanh))
        return total * (grad * gain[...]), value * rstd - xh_b

    sums = [jnp.zeros((8, CH), F32)] * 2
    for i in range(4):
        r = 1 + 2 * i
        w, xhat = back([(r, 2)])
        wgr[r : r + 2] = w.reshape(2, 8, 16, CH)
        sums[0] = sums[0] + jnp.sum(w.reshape(32, 8, CH), axis=0)
        sums[1] = sums[1] + jnp.sum((w * xhat).reshape(32, 8, CH), axis=0)
    pack(p3, sums)
    ex3 = exchange(2, p3)
    w, _ = back([(0, 1), (9, 1)])
    wgr[0:1] = w[:128].reshape(1, 8, 16, CH)
    wgr[9:10] = w[128:].reshape(1, 8, 16, CH)

    stats = group_total(collect(p3, ex3)) / GROUP_N
    mean_w = as_row(stats, 0)
    mean_x = as_row(stats, 4)
    coef_f = -rstd * rstd * mean_x
    coef_0 = (xh_b * mean_x - mean_w) * rstd

    def first_row(r, carry):
        value = wgr[r] * rstd + first[r + 2] * coef_f + coef_0
        value = (value * inside(8 * j - 1 + r)).astype(BF)
        start = pl.multiple_of(r * 16, 16)
        for o in range(8):
            gfc[pl.ds(start, 16), o * CH : (o + 1) * CH] = value[o]
        return carry

    lax.fori_loop(0, 10, first_row, 0)
    back_y = mm_nt(gfc[...], wb[...])
    grad_lat = jnp.zeros((128, 128), F32)
    edge = jnp.zeros((128, 128), F32)
    lane = iota((128, 128), 1)
    blk = iota((128, 128), 0) & 15
    for dy in range(3):
        start = (2 - dy) * 16
        grad_lat = grad_lat + back_y[start : start + 128, dy * 128 : dy * 128 + 128]
        part = back_y[start : start + 128, 384:512]
        part = jnp.where((lane >> 5) == dy, part, 0.0)
        edge = edge + pltpu.roll(part, (112 - 32 * dy) % 128, 1)
    grad_lat = grad_lat + jnp.where((lane >= 112) & (blk < 15), pltpu.roll(edge, 127, 0), 0.0)
    grad_lat = grad_lat + jnp.where((lane < 16) & (blk > 0), pltpu.roll(edge, 1, 0), 0.0)
    sigma = noise_level(time_ref[zh], (128, 128))
    gvx[c] = (-sigma * (grad_lat / LSCALE)).astype(BF).reshape(2, 64, 128)

    gv_pair = pltpu.make_async_remote_copy(
        src_ref=gvx.at[c], dst_ref=gvx.at[c], send_sem=gx_s, recv_sem=gx_r,
        device_id={"grp": 1 - c}, device_id_type=MESH,
    )
    gv_pair.start()

    def gv_copy(e):
        copy = pltpu.make_async_remote_copy(
            src_ref=gvx.at[c, e], dst_ref=gvr.at[zh],
            send_sem=gv_s.at[e], recv_sem=gv_r.at[zh],
            device_id={"tok": y * 2 + c, "grp": e}, device_id_type=MESH,
        )
        return copy, jnp.logical_not((c == zh) & (c == e))

    for e in range(2):
        copy, ok = gv_copy(e)
        pl.when(ok)(copy.start)

    @pl.when(c == zh)
    def _():
        gvr[zh] = gvx[c, c]

    def tokens(parts):
        for a in range(2):
            rows = [
                part[(2 * p + a) * 16 : (2 * p + a) * 16 + 16, :] for part in parts for p in range(2)
            ]
            full = jnp.concatenate(rows, axis=0).astype(F32)
            for chi in range(4):
                ve[a, pl.ds(chi, 64, stride=4), :] = jnp.where(lane_chi == chi, full, 0.0)
        return jnp.concatenate([ve[0], ve[1]], axis=1).astype(BF)

    j_r, k_c = iota((256, 256), 0), iota((256, 256), 1)
    target_lane = j_r & 63
    keep = ((target_lane >> 5) == (k_c >> 7)) & ((target_lane & 31) == (k_c & 31))
    quad = one_hot(keep & ((j_r < 64) | (j_r >= 192)))
    for copy in mod_copies:
        copy.wait_recv()

    def term_of(row):
        grads = mm_nt(tokens([gvx[row, 0], gvx[row, 1]]), quad).astype(BF)
        lanes = pl.ds(pl.multiple_of(row * 256, 256), 256)
        return mm(modp[0:608, lanes], grads[:, :128]) + mm(modp[608:1216, lanes], grads[:, 128:])

    wt[...] = term_of(c) * (1.0 / 2048.0)
    gv_pair.wait_recv()
    wt[...] += term_of(1 - c) * (1.0 / 2048.0)
    for k in range(16):
        s1send[k, 0:32, :] = wt[38 * k : 38 * k + 32, :].astype(BF)
        tail = jnp.concatenate([wt[38 * k + 32 : 38 * k + 38, :], jnp.zeros((10, 128), F32)], axis=0)
        s1send[k, 32:48, :] = tail.astype(BF)
    me_xy = x * 4 + y
    s1 = []
    for d in range(1, 16):
        n = lax.rem(me_xy + d, 16)
        s1.append(
            pltpu.make_async_remote_copy(
                src_ref=s1send.at[n], dst_ref=s1recv.at[me_xy],
                send_sem=s1_s.at[d - 1], recv_sem=s1_r.at[d - 1],
                device_id={"batch": zl * 4 + lax.div(n, 4), "tok": lax.rem(n, 4) * 2 + zh},
                device_id_type=MESH,
            )
        )
    for copy in s1:
        copy.start()
    s1recv[me_xy] = s1send[me_xy]

    for h in range(2):
        copy = pltpu.make_async_remote_copy(
            src_ref=gvx.at[0, 0], dst_ref=gvr.at[h],
            send_sem=gv_s.at[0], recv_sem=gv_r.at[h],
            device_id={"tok": y * 2 + c, "grp": 0}, device_id_type=MESH,
        )
        pl.when(jnp.logical_not((c == zh) & (zh == h)))(copy.wait_recv)
    own_tokens[...] = tokens([gvr[0], gvr[1]])

    def hidden_rows(i, carry):
        img, start = lax.div(i, 4), pl.multiple_of(lax.rem(i, 4) * 32, 32)
        flat = pl.multiple_of(i * 32, 32)
        grad_mod = mm(own_tokens[pl.ds(flat, 32), :], wrep[...])
        inv = stat_i[pl.ds(flat, 32), :]
        normal = (hid[img, pl.ds(start, 32), :].astype(F32) - stat_m[pl.ds(flat, 32), :]) * inv
        e = grad_mod * (1.0 + scalev[pl.ds(img, 1), :])
        mean_e = jnp.sum(e, axis=-1, keepdims=True) / D
        mean_n = jnp.sum(e * normal, axis=-1, keepdims=True) / D
        hgv[img, pl.ds(start, 32), :] = (inv * (e - mean_e - normal * mean_n)).astype(BF)
        return carry

    lax.fori_loop(0, 8, hidden_rows, 0)

    for copy in s1:
        copy.wait_recv()
    total = s1recv[0].astype(F32)
    for k in range(1, 16):
        total = total + s1recv[k].astype(F32)
    wt[0:48, :] = total
    for z in range(2):
        s2send[z] = wt[19 * z : 19 * z + 24, :]
    me_z = zl * 2 + zh

    def line_copy(n):
        dest_zl, dest_zh, dest_c = 2 * c + n // 4, (n // 2) % 2, n % 2
        copy = pltpu.make_async_remote_copy(
            src_ref=s2send.at[dest_zh], dst_ref=s2recv.at[me_z],
            send_sem=s2_s.at[n], recv_sem=s2_r.at[me_z],
            device_id={"batch": dest_zl * 4 + x, "tok": y * 2 + dest_zh, "grp": dest_c},
            device_id_type=MESH,
        )
        return copy, jnp.logical_not((dest_zl == zl) & (dest_zh == zh) & (dest_c == c))

    for n in range(8):
        copy, ok = line_copy(n)
        pl.when(ok)(copy.start)
    self_line = lax.div(zl, 2) == c

    @pl.when(self_line)
    def _():
        s2recv[me_z] = s2send[zh]

    for copy in pix_copies:
        copy.wait_recv()
    l384, k384 = iota((384, 384), 0), iota((384, 384), 1)
    cell = l384 & 127
    place = jnp.where(k384 == ((cell & 15) * 8 + (cell >> 4)) * 3 + (l384 >> 7), 1.0, 0.0)
    for i in range(2):
        slab = map_ref[i]
        block = pixg[i, slab >> 1]
        odd = jnp.full((24, 128), slab & 1, jnp.int32) == 1
        block = jnp.where(odd, pltpu.roll(block, 20, 0), block)
        wide = jnp.concatenate([block[0:8], block[8:16], block[16:24]], axis=1)
        moved = lax.dot_general(
            wide, place, (((1,), (0,)), ((), ())),
            precision=lax.Precision.HIGHEST, preferred_element_type=F32,
        )
        pix_out[i, 0] = moved[0:4]

    rew_copy.wait_recv()
    lane = iota((1, 128), 1)
    rew_out[...] = jnp.where(lane == 0, rewb[0, 0:1, :], rewb[1, 0:1, :])[:, 0:2]

    for n in range(8):
        copy = pltpu.make_async_remote_copy(
            src_ref=s2send.at[0], dst_ref=s2recv.at[n],
            send_sem=s2_s.at[0], recv_sem=s2_r.at[n],
            device_id={"grp": 1 - c}, device_id_type=MESH,
        )
        pl.when(jnp.logical_not(self_line & (me_z == n)))(copy.wait_recv)
    total = s2recv[0]
    for k in range(1, 8):
        total = total + s2recv[k]
    odd = jnp.full((24, 128), lax.rem(zl, 2), jnp.int32) == 1
    total = jnp.where(odd, pltpu.roll(total, 64, 1), total)
    wg_ref[...] = total[0:19, 0:64]

    for h in range(2):
        for copy, ok in lat_copies(h):
            pl.when(ok)(copy.wait_send)
    for copy in ex1 + ex2 + ex3 + pix_copies + s1 + mod_copies + [rew_copy, gv_pair]:
        copy.wait_send()
    for e in range(2):
        copy, ok = gv_copy(e)
        pl.when(ok)(copy.wait_send)
    for n in range(8):
        copy, ok = line_copy(n)
        pl.when(ok)(copy.wait_send)


def hand_out(*refs):
    sem = refs[8]
    copies = [pltpu.make_async_copy(refs[i], refs[4 + i], sem.at[i]) for i in range(4)]
    for copy in copies:
        copy.start()
    for copy in copies:
        copy.wait()


def local(
    hidden, shift, scale, out_weight, noisy_latent, timestep, in_kernel, in_bias,
    norm_gain, norm_bias, mid_kernel, mid_bias, rgb_weight, clip_weight, text_embed, slab_map,
):
    any_spec = pl.BlockSpec(memory_space=pl.ANY)
    smem = pl.BlockSpec(memory_space=pltpu.SMEM)
    vmem = pl.BlockSpec(memory_space=pltpu.VMEM)
    dma = pltpu.SemaphoreType.DMA

    def v(dtype, *shape):
        return pltpu.VMEM(shape, dtype)

    hg, wg, reward, pixels = pl.pallas_call(
        kernel,
        out_shape=(
            pltpu.VMEM((2, 128, D), BF),
            pltpu.VMEM((19, 64), F32),
            pltpu.VMEM((1, 2), F32),
            pltpu.VMEM((2, 1, 4, 384), F32),
        ),
        in_specs=[smem, smem] + [any_spec] * 14,
        out_specs=(vmem, vmem, vmem, vmem),
        scratch_shapes=[
            v(BF, 2, 128, D), v(F32, 2, D), v(F32, 2, D), v(BF, 64, D), v(F32, 2, 4, 2048),
            v(BF, 3, 3, 16, CH), v(F32, 1, CH), v(F32, 1, CH), v(F32, 1, CH),
            v(BF, 3, 3, CH, CH), v(F32, 1, CH), v(BF, 3, CH), v(BF, CH, EMB), v(F32, 2, EMB),
            v(F32, 256, 1), v(F32, 256, 1), v(BF, 256, D), v(BF, 2, D, 128), v(BF, D // 2, 512),
            v(BF, 256, D), v(F32, 2, 256, 128), v(F32, 2, 4, 16, 128), v(BF, 2, 64, 128),
            v(BF, 4, 64, 128), v(BF, 224, 512), v(BF, 512, 8 * CH),
            v(F32, 14, 8, 16, CH), v(BF, 14, 10, 16, CH), v(F32, 12, 8, 16, CH),
            v(BF, 12, 10, 16, CH), v(F32, 10, 8, 16, CH), v(BF, 160, 8 * CH), v(F32, 8, 128),
            v(F32, 8, 8, 128), v(F32, 8, 8, 128), v(F32, 8, 8, 128), v(F32, 2, 8, 128),
            v(F32, 2, 8, 24, 128), v(BF, 2, 2, 64, 128), v(BF, 2, 64, 128), v(F32, 608, 128),
            v(BF, 16, 48, 128), v(BF, 16, 48, 128), v(F32, 2, 24, 128), v(F32, 8, 24, 128),
            v(BF, 256, 256),
            dma((14,)), dma((4,)), dma((4,)), dma((3, 7)), dma((3, 7)), dma((15,)), dma((15,)),
            dma, dma, dma((3,)), dma((3,)), dma, dma, dma((2,)), dma((2,)), dma((15,)), dma((15,)), dma((8,)), dma((8,)),
        ],
        compiler_params=pltpu.CompilerParams(
            collective_id=0, has_side_effects=True, vmem_limit_bytes=58 * 2**20
        ),
    )(
        timestep, slab_map.reshape(2), hidden, shift, scale, out_weight.T, noisy_latent, in_kernel,
        in_bias.reshape(1, CH), norm_gain.reshape(1, CH), norm_bias.reshape(1, CH),
        mid_kernel, mid_bias.reshape(1, CH), rgb_weight.T, clip_weight, text_embed,
    )
    hg, wg, reward, pixels = pl.pallas_call(
        hand_out,
        out_shape=(
            jax.ShapeDtypeStruct((2, 128, D), BF),
            jax.ShapeDtypeStruct((19, 64), F32),
            jax.ShapeDtypeStruct((1, 2), F32),
            jax.ShapeDtypeStruct((2, 1, 4, 384), F32),
        ),
        in_specs=[vmem] * 4,
        out_specs=[any_spec] * 4,
        scratch_shapes=[dma((4,))],
    )(hg, wg, reward, pixels)
    return hg, wg, reward.reshape(2), pixels


def solution(mesh):
    rows = ("tok", "grp")
    return jax.shard_map(
        local,
        mesh=mesh,
        in_specs=(
            P("batch", rows, None), P("batch", None), P("batch", None), P(),
            P("batch", rows, None), P("batch"), P(), P(), P(), P(), P(), P(), P(), P(),
            P("batch", None), P("batch", rows),
        ),
        out_specs=(
            P("batch", rows, None), P(("batch", "tok"), None), P("batch"),
            P("batch", rows, None, None),
        ),
        check_vma=False,
    )
```

```python
import jax
import jax.numpy as jnp
from jax import lax
from jax.experimental import pallas as pl
from jax.experimental.pallas import tpu as pltpu
from jax.sharding import PartitionSpec as P

D = 2432
CH = 512
EMB = 1024
GROUP_N = 131072.0
CELLS = 8192.0
EPS = 1e-6
LSCALE = 1.5305
LSHIFT = 0.0609
REWARD_W = 16.0
BF = jnp.bfloat16
F32 = jnp.float32
MESH = pl.DeviceIdType.MESH

NT = (((1,), (1,)), ((), ()))


def mm(a, b):
    return jnp.dot(a, b, preferred_element_type=F32)


def mm_nt(a, b):
    return lax.dot_general(a, b, NT, preferred_element_type=F32)


def iota(shape, dim):
    return lax.broadcasted_iota(jnp.int32, shape, dim)


def one_hot(cond):
    return jnp.where(cond, 1.0, 0.0).astype(BF)


def noise_level(step, shape):
    fraction = (jnp.full(shape, step, jnp.int32).astype(F32) + 1.0) / 1000.0
    return 3.0 * fraction / (1.0 + 2.0 * fraction)


def group_total(tile):
    lane = iota(tile.shape, 1)
    for step in (1, 2, 4, 8):
        tile = tile + jnp.where(
            (lane & step) != 0, pltpu.roll(tile, step, 1), pltpu.roll(tile, 128 - step, 1)
        )
    return tile


def kernel(
    time_ref, map_ref,
    hidden_h, shift_h, scale_h, outw_h, noisy_h, ink_h, inb_h, gain_h, nbias_h,
    midk_h, midb_h, rgb_h, clip_h, text_h,
    hgv, wg_ref, rew_out, pix_out,
    hid, shiftv, scalev, outw, noisy, ink, inb, gain, nbias, midk, midb, rgb, clip, text,
    stat_m, stat_i, mod, modt, modp, wrep, ve, nl, latsend, rbuf, lhs, wb,
    first, act, slope, gsec, wgr, gfc, rowbuf,
    p1, p2, p3, rewb, pixg, gvx, gvr, wt, s1send, s1recv, s2send, s2recv, own_tokens,
    load_sem, lat_s, lat_r, ex_s, ex_r, pix_s, pix_r, rew_s, rew_r, mod_s, mod_r,
    gx_s, gx_r, gv_s, gv_r, s1_s, s1_r, s2_s, s2_r,
):
    bt = lax.axis_index("batch")
    tok = lax.axis_index("tok")
    c = lax.axis_index("grp")
    y, zh = lax.div(tok, 2), lax.rem(tok, 2)
    zl, x = lax.div(bt, 4), lax.rem(bt, 4)
    j = 2 * y + c

    pairs = [
        (outw_h, outw), (scale_h, scalev), (shift_h, shiftv), (hidden_h, hid),
        (noisy_h, noisy), (ink_h, ink), (inb_h, inb), (gain_h, gain), (nbias_h, nbias),
        (midb_h, midb), (rgb_h, rgb), (midk_h, midk), (clip_h, clip), (text_h, text),
    ]
    loads = [
        pltpu.make_async_copy(src, dst, load_sem.at[i]) for i, (src, dst) in enumerate(pairs)
    ]
    for copy in loads[:4]:
        copy.start()

    bar = pltpu.get_barrier_semaphore()

    def greet(**where):
        pl.semaphore_signal(bar, inc=1, device_id=where, device_id_type=MESH)

    for d in range(15, 0, -1):
        n = lax.rem(tok * 2 + c + d, 16)
        greet(tok=lax.div(n, 2), grp=lax.rem(n, 2))
    for dz in range(1, 4):
        for n in range(4):
            greet(batch=lax.rem(zl + dz, 4) * 4 + x, tok=y * 2 + n // 2, grp=n % 2)
    for dx in range(1, 4):
        for dy in range(4):
            greet(batch=zl * 4 + lax.rem(x + dx, 4), tok=lax.rem(y + dy, 4) * 2 + zh)
    for copy in loads[4:]:
        copy.start()

    loads[0].wait()
    j256, k64 = iota((256, 64), 0), iota((256, 64), 1)
    spread = one_hot(((k64 >> 5) == (j256 >> 7)) & ((k64 & 31) == (j256 & 31)))
    wrep[...] = mm(spread, outw[...]).astype(BF)

    for copy in loads[1:4]:
        copy.wait()

    def norm_rows(i, carry):
        img, start = lax.div(i, 4), pl.multiple_of(lax.rem(i, 4) * 32, 32)
        flat = pl.multiple_of(i * 32, 32)
        values = hid[img, pl.ds(start, 32), :].astype(F32)
        mean = jnp.sum(values, axis=-1, keepdims=True) / D
        centered = values - mean
        inv = lax.rsqrt(jnp.sum(centered * centered, axis=-1, keepdims=True) / D + EPS)
        stat_m[pl.ds(flat, 32), :] = mean
        stat_i[pl.ds(flat, 32), :] = inv
        gain_row = 1.0 + scalev[pl.ds(img, 1), :]
        mod[pl.ds(flat, 32), :] = (
            centered * inv * gain_row + shiftv[pl.ds(img, 1), :]
        ).astype(BF)
        return carry

    lax.fori_loop(0, 8, norm_rows, 0)
    velocity = mm_nt(mod[...], wrep[...])
    for a in range(2):
        ve[a] = velocity[:, a * 128 : a * 128 + 128]

    loads[4].wait()
    for i in range(2):
        for b in range(16):
            nl[i, :, b, :] = noisy[i, :, b * 128 : (b + 1) * 128]
    lane_chi = iota((64, 128), 1) >> 5
    vel = [jnp.zeros((64, 128), F32)] * 2
    for chi in range(4):
        for a in range(2):
            vel[a] = jnp.where(lane_chi == chi, ve[a, pl.ds(chi, 64, stride=4), :], vel[a])
    for i in range(2):
        sigma = noise_level(time_ref[i], (16, 128))
        for p in range(2):
            for a in range(2):
                r = 2 * p + a
                part = vel[a][(i * 2 + p) * 16 : (i * 2 + p) * 16 + 16, :]
                latsend[i, r * 16 : r * 16 + 16, :] = (
                    (nl[i, r] - sigma * part) / LSCALE + LSHIFT
                ).astype(BF)

    pl.semaphore_wait(bar, 39)

    main_pos = 1 + c
    halo_j = 2 * y + zh + 2 * c - 1
    halo_pos = 3 - 3 * c
    halo_ok = (halo_j >= 0) & (halo_j <= 7)
    self_main = c == zh

    def lat_copies(h):
        here = zh == h
        main = pltpu.make_async_remote_copy(
            src_ref=latsend.at[h], dst_ref=rbuf.at[main_pos],
            send_sem=lat_s.at[2 * h], recv_sem=lat_r.at[main_pos],
            device_id={"tok": y * 2 + h, "grp": zh}, device_id_type=MESH,
        )
        halo = pltpu.make_async_remote_copy(
            src_ref=latsend.at[h], dst_ref=rbuf.at[halo_pos],
            send_sem=lat_s.at[2 * h + 1], recv_sem=lat_r.at[halo_pos],
            device_id={"tok": lax.div(halo_j, 2) * 2 + h, "grp": lax.rem(halo_j, 2)},
            device_id_type=MESH,
        )
        main_ok = jnp.logical_not(here & self_main)
        far_ok = halo_ok & jnp.logical_not(here & jnp.logical_not(self_main))
        return (main, main_ok), (halo, far_ok)

    for h in range(2):
        for copy, ok in lat_copies(h):
            pl.when(ok)(copy.start)
    self_pos = jnp.where(self_main, main_pos, halo_pos)
    rbuf[self_pos] = latsend[zh]

    @pl.when(j == 0)
    def _():
        rbuf[0] = jnp.zeros((64, 128), BF)

    @pl.when(j == 7)
    def _():
        rbuf[3] = jnp.zeros((64, 128), BF)

    def flip(k, carry):
        start = pl.multiple_of(k * 128, 128)
        for h in range(2):
            block = mod[h * 128 : h * 128 + 128, pl.ds(start, 128)]
            modt[h, pl.ds(start, 128), :] = block.astype(F32).T.astype(BF)
        return carry

    lax.fori_loop(0, 19, flip, 0)
    half = D // 2
    place4 = zh * 2 + c
    mod_lane = pl.ds(pl.multiple_of(place4 * 128, 128), 128)
    modp[:, mod_lane] = modt[zh, pl.ds(pl.multiple_of(c * half, 64), half), :]
    mod_copies = []
    for d in range(1, 4):
        n = lax.rem(place4 + d, 4)
        h, core = lax.div(n, 2), lax.rem(n, 2)
        for part, (low, size) in enumerate(((0, 608), (608, 608))):
            mod_copies.append(
                pltpu.make_async_remote_copy(
                    src_ref=modt.at[h, pl.ds(pl.multiple_of(core * half + low, 32), size), :],
                    dst_ref=modp.at[low : low + size, mod_lane],
                    send_sem=mod_s.at[part, d - 1], recv_sem=mod_r.at[part, d - 1],
                    device_id={"tok": y * 2 + h, "grp": core}, device_id_type=MESH,
                )
            )
    for copy in mod_copies:
        copy.start()

    for copy in loads[5:11]:
        copy.wait()

    def clear(i, carry):
        wb[pl.ds(pl.multiple_of(i * 16, 16), 16), :] = jnp.zeros((16, 8 * CH), BF)
        return carry

    lax.fori_loop(0, 32, clear, 0)
    for dy in range(3):
        for dx in range(3):
            tap = ink[dy, dx]
            for o in range(8):
                i = o + dx - 1
                row = 384 + 32 * dy if i < 0 else 384 + 32 * dy + 16 if i > 7 else dy * 128 + 16 * i
                wb[row : row + 16, o * CH : (o + 1) * CH] = tap
    rgbt = mm(one_hot(iota((8, 3), 0) == iota((8, 3), 1)), rgb[...]).astype(BF)

    def wait_lat(pos, ok):
        copy = pltpu.make_async_remote_copy(
            src_ref=latsend.at[0], dst_ref=rbuf.at[pos],
            send_sem=lat_s.at[0], recv_sem=lat_r.at[pos],
            device_id={"tok": tok, "grp": 1 - c}, device_id_type=MESH,
        )
        pl.when(ok & (self_pos != pos))(copy.wait_recv)

    wait_lat(0, j > 0)
    wait_lat(1, j >= 0)
    wait_lat(2, j >= 0)
    wait_lat(3, j < 7)

    lat = rbuf[...].reshape(256, 128)
    lat32 = lat.astype(F32)
    blk = iota((256, 128), 0) & 15
    lane = iota((256, 128), 1)
    after = jnp.where((lane < 16) & (blk < 15), pltpu.roll(lat32, 255, 0), 0.0)
    before = jnp.where((lane >= 112) & (blk > 0), pltpu.roll(lat32, 1, 0), 0.0)
    edge = after + before
    side = sum(
        pltpu.roll(edge, 16 + 32 * dy, 1)[16 * dy : 16 * dy + 224] for dy in range(3)
    )
    for dy in range(3):
        lhs[:, dy * 128 : dy * 128 + 128] = lat[16 * dy : 16 * dy + 224]
    lhs[:, 384:512] = side.astype(BF)

    sum_one = jnp.zeros((8, CH), F32)
    sum_two = jnp.zeros((8, CH), F32)
    for o in range(8):
        out = mm(lhs[48:176, :], wb[:, o * CH : (o + 1) * CH]) + inb[...]
        first[3:11, o] = out.reshape(8, 16, CH)
        own = out.reshape(16, 8, CH)
        sum_one = sum_one + jnp.sum(own, axis=0)
        sum_two = sum_two + jnp.sum(own * own, axis=0)

    def pack(buf, rows):
        for n, row in enumerate(rows):
            row = jnp.sum(row, axis=0, keepdims=True)
            for k in range(4):
                buf[j, n * 4 + k : n * 4 + k + 1, :] = row[:, k * 128 : k * 128 + 128]

    def exchange(phase, buf):
        copies = []
        for d in range(1, 8):
            n = lax.rem(j + d, 8)
            copies.append(
                pltpu.make_async_remote_copy(
                    src_ref=buf.at[j], dst_ref=buf.at[j],
                    send_sem=ex_s.at[phase, d - 1], recv_sem=ex_r.at[phase, d - 1],
                    device_id={"tok": lax.div(n, 2) * 2 + zh, "grp": lax.rem(n, 2)},
                    device_id_type=MESH,
                )
            )
        for copy in copies:
            copy.start()
        return copies

    def collect(buf, copies):
        for copy in copies:
            copy.wait_recv()
        total = buf[0]
        for k in range(1, 8):
            total = total + buf[k]
        return total

    def as_row(tile, start):
        rowbuf[...] = tile
        return jnp.concatenate([rowbuf[start + k : start + k + 1, :] for k in range(4)], axis=1)

    pack(p1, (sum_one, sum_two))
    ex1 = exchange(0, p1)
    beside = jnp.concatenate([lhs[0:48, :], lhs[176:224, :]], axis=0)
    for o in range(8):
        out = (mm(beside, wb[:, o * CH : (o + 1) * CH]) + inb[...]).reshape(6, 16, CH)
        first[0:3, o] = out[0:3]
        first[11:14, o] = out[3:6]

    stats = group_total(collect(p1, ex1)) / GROUP_N
    mu = as_row(stats, 0)
    rstd = lax.rsqrt(as_row(stats, 4) - mu * mu + EPS)
    coef_a = rstd * gain[...] * 0.5
    coef_b = (nbias[...] - mu * rstd * gain[...]) * 0.5

    blk16 = iota((16, CH), 0)

    def put_row(buf, r, value):
        buf[r, 1:9] = value.astype(BF)
        buf[r, 0] = jnp.where(blk16 > 0, pltpu.roll(value[7], 1, 0), 0.0).astype(BF)
        buf[r, 9] = jnp.where(blk16 < 15, pltpu.roll(value[0], 15, 0), 0.0).astype(BF)

    def inside(row):
        return ((row >= 0) & (row < 64)).astype(F32)

    def act_row(r, carry):
        half_u = first[r] * coef_a + coef_b
        value = half_u * (1.0 + jnp.tanh(half_u)) * inside(8 * j - 3 + r)
        put_row(act, r, value)
        return carry

    lax.fori_loop(0, 14, act_row, 0)

    loads[11].wait()

    def decode(pieces):
        total = None
        for dy in range(3):
            for dx in range(3):
                part = [act[pl.ds(r + dy, n), dx : dx + 8].reshape(n * 128, CH) for r, n in pieces]
                part = part[0] if len(part) == 1 else jnp.concatenate(part, axis=0)
                term = mm(part, midk[dy, dx])
                total = term if total is None else total + term
        half_u = (total + midb[...]) * 0.5
        tanh = jnp.tanh(half_u)
        grad = 0.5 * ((1.0 + tanh) + half_u * (1.0 - tanh * tanh))
        return half_u * (1.0 + tanh), grad

    def own_decode(i, total):
        r = 2 + 4 * i
        value, grad = decode([(r, 4)])
        slope[pl.ds(r, 4)] = grad.reshape(4, 8, 16, CH)
        pixel = mm_nt(rgbt, value.astype(BF))
        for colour in range(3):
            for row in range(4):
                pixg[zh, j, pl.ds(colour * 8 + 4 * i + row, 1), :] = (
                    pixel[colour : colour + 1, row * 128 : row * 128 + 128]
                )
        return total + jnp.sum(value.reshape(64, 8, CH), axis=0)

    pooled_sum = lax.fori_loop(0, 2, own_decode, jnp.zeros((8, CH), F32))
    pack(p2, (pooled_sum,))
    ex2 = exchange(1, p2)

    pix_copies = []
    for d in range(1, 16):
        n = lax.rem(tok * 2 + c + d, 16)
        pix_copies.append(
            pltpu.make_async_remote_copy(
                src_ref=pixg.at[zh, j], dst_ref=pixg.at[zh, j],
                send_sem=pix_s.at[d - 1], recv_sem=pix_r.at[d - 1],
                device_id={"tok": lax.div(n, 2), "grp": lax.rem(n, 2)}, device_id_type=MESH,
            )
        )

    _, grad = decode([(0, 2), (10, 2)])
    slope[0:2] = grad[:256].reshape(2, 8, 16, CH)
    slope[10:12] = grad[256:].reshape(2, 8, 16, CH)

    loads[12].wait()
    loads[13].wait()
    pooled = (as_row(collect(p2, ex2), 0) / CELLS).astype(BF)
    for copy in pix_copies:
        copy.start()
    feature = mm(jnp.broadcast_to(pooled, (8, CH)), clip[...])
    target = text[pl.ds(zh, 1), :]
    norm_f = jnp.sqrt(jnp.sum(feature * feature, axis=-1, keepdims=True) + EPS)
    norm_t = jnp.sqrt(jnp.sum(target * target, axis=-1, keepdims=True) + EPS)
    reward = jnp.sum(feature * target, axis=-1, keepdims=True) / (norm_f * norm_t)
    grad_feature = (
        REWARD_W * (target / (norm_f * norm_t) - reward * feature / (norm_f * norm_f))
    ).astype(BF)
    grad_act = mm_nt(grad_feature, clip[...])[0:1, :]
    rewb[zh] = jnp.broadcast_to(reward, (8, 128))
    rew_copy = pltpu.make_async_remote_copy(
        src_ref=rewb.at[zh], dst_ref=rewb.at[zh], send_sem=rew_s, recv_sem=rew_r,
        device_id={"tok": y * 2 + 1 - zh}, device_id_type=MESH,
    )
    rew_copy.start()

    def grad_row(r, carry):
        put_row(gsec, r, slope[r] * grad_act * inside(8 * j - 2 + r))
        return carry

    lax.fori_loop(0, 12, grad_row, 0)

    xh_b = mu * rstd

    def back(pieces):
        total = None
        for dy in range(3):
            for dx in range(3):
                part = [
                    gsec[pl.ds(r + 2 - dy, n), 2 - dx : 10 - dx].reshape(n * 128, CH)
                    for r, n in pieces
                ]
                part = part[0] if len(part) == 1 else jnp.concatenate(part, axis=0)
                term = mm_nt(part, midk[dy, dx])
                total = term if total is None else total + term
        value = [first[pl.ds(r + 2, n)].reshape(n * 128, CH) for r, n in pieces]
        value = value[0] if len(value) == 1 else jnp.concatenate(value, axis=0)
        half_u = value * coef_a + coef_b
        tanh = jnp.tanh(half_u)
        grad = 0.5 * ((1.0 + tanh) + half_u * (1.0 - tanh * tanh))
        return total * (grad * gain[...]), value * rstd - xh_b

    def own_back(i, carry):
        r = 1 + 4 * i
        w, xhat = back([(r, 4)])
        wgr[pl.ds(r, 4)] = w.reshape(4, 8, 16, CH)
        return (
            carry[0] + jnp.sum(w.reshape(64, 8, CH), axis=0),
            carry[1] + jnp.sum((w * xhat).reshape(64, 8, CH), axis=0),
        )

    zero = jnp.zeros((8, CH), F32)
    sums = lax.fori_loop(0, 2, own_back, (zero, zero))
    pack(p3, sums)
    ex3 = exchange(2, p3)
    w, _ = back([(0, 1), (9, 1)])
    wgr[0:1] = w[:128].reshape(1, 8, 16, CH)
    wgr[9:10] = w[128:].reshape(1, 8, 16, CH)

    stats = group_total(collect(p3, ex3)) / GROUP_N
    mean_w = as_row(stats, 0)
    mean_x = as_row(stats, 4)
    coef_f = -rstd * rstd * mean_x
    coef_0 = (xh_b * mean_x - mean_w) * rstd

    def first_row(r, carry):
        value = wgr[r] * rstd + first[r + 2] * coef_f + coef_0
        value = (value * inside(8 * j - 1 + r)).astype(BF)
        start = pl.multiple_of(r * 16, 16)
        for o in range(8):
            gfc[pl.ds(start, 16), o * CH : (o + 1) * CH] = value[o]
        return carry

    lax.fori_loop(0, 10, first_row, 0)
    back_y = mm_nt(gfc[...], wb[...])
    grad_lat = jnp.zeros((128, 128), F32)
    edge = jnp.zeros((128, 128), F32)
    lane = iota((128, 128), 1)
    blk = iota((128, 128), 0) & 15
    for dy in range(3):
        start = (2 - dy) * 16
        grad_lat = grad_lat + back_y[start : start + 128, dy * 128 : dy * 128 + 128]
        part = back_y[start : start + 128, 384:512]
        part = jnp.where((lane >> 5) == dy, part, 0.0)
        edge = edge + pltpu.roll(part, (112 - 32 * dy) % 128, 1)
    grad_lat = grad_lat + jnp.where((lane >= 112) & (blk < 15), pltpu.roll(edge, 127, 0), 0.0)
    grad_lat = grad_lat + jnp.where((lane < 16) & (blk > 0), pltpu.roll(edge, 1, 0), 0.0)
    sigma = noise_level(time_ref[zh], (128, 128))
    gvx[c] = (-sigma * (grad_lat / LSCALE)).astype(BF).reshape(2, 64, 128)

    gv_pair = pltpu.make_async_remote_copy(
        src_ref=gvx.at[c], dst_ref=gvx.at[c], send_sem=gx_s, recv_sem=gx_r,
        device_id={"grp": 1 - c}, device_id_type=MESH,
    )
    gv_pair.start()

    def gv_copy(e):
        copy = pltpu.make_async_remote_copy(
            src_ref=gvx.at[c, e], dst_ref=gvr.at[zh],
            send_sem=gv_s.at[e], recv_sem=gv_r.at[zh],
            device_id={"tok": y * 2 + c, "grp": e}, device_id_type=MESH,
        )
        return copy, jnp.logical_not((c == zh) & (c == e))

    for e in range(2):
        copy, ok = gv_copy(e)
        pl.when(ok)(copy.start)

    @pl.when(c == zh)
    def _():
        gvr[zh] = gvx[c, c]

    def tokens(parts):
        for a in range(2):
            rows = [
                part[(2 * p + a) * 16 : (2 * p + a) * 16 + 16, :] for part in parts for p in range(2)
            ]
            full = jnp.concatenate(rows, axis=0).astype(F32)
            for chi in range(4):
                ve[a, pl.ds(chi, 64, stride=4), :] = jnp.where(lane_chi == chi, full, 0.0)
        return jnp.concatenate([ve[0], ve[1]], axis=1).astype(BF)

    j_r, k_c = iota((256, 256), 0), iota((256, 256), 1)
    target_lane = j_r & 63
    keep = ((target_lane >> 5) == (k_c >> 7)) & ((target_lane & 31) == (k_c & 31))
    quad = one_hot(keep & ((j_r < 64) | (j_r >= 192)))
    for copy in mod_copies:
        copy.wait_recv()

    def term_of(row):
        grads = mm_nt(tokens([gvx[row, 0], gvx[row, 1]]), quad).astype(BF)
        lanes = pl.ds(pl.multiple_of(row * 256, 256), 256)
        return mm(modp[0:608, lanes], grads[:, :128]) + mm(modp[608:1216, lanes], grads[:, 128:])

    wt[...] = term_of(c) * (1.0 / 2048.0)
    gv_pair.wait_recv()
    wt[...] += term_of(1 - c) * (1.0 / 2048.0)
    for k in range(16):
        s1send[k, 0:32, :] = wt[38 * k : 38 * k + 32, :].astype(BF)
        tail = jnp.concatenate([wt[38 * k + 32 : 38 * k + 38, :], jnp.zeros((10, 128), F32)], axis=0)
        s1send[k, 32:48, :] = tail.astype(BF)
    me_xy = x * 4 + y
    s1 = []
    for d in range(1, 16):
        n = lax.rem(me_xy + d, 16)
        s1.append(
            pltpu.make_async_remote_copy(
                src_ref=s1send.at[n], dst_ref=s1recv.at[me_xy],
                send_sem=s1_s.at[d - 1], recv_sem=s1_r.at[d - 1],
                device_id={"batch": zl * 4 + lax.div(n, 4), "tok": lax.rem(n, 4) * 2 + zh},
                device_id_type=MESH,
            )
        )
    for copy in s1:
        copy.start()
    s1recv[me_xy] = s1send[me_xy]

    for h in range(2):
        copy = pltpu.make_async_remote_copy(
            src_ref=gvx.at[0, 0], dst_ref=gvr.at[h],
            send_sem=gv_s.at[0], recv_sem=gv_r.at[h],
            device_id={"tok": y * 2 + c, "grp": 0}, device_id_type=MESH,
        )
        pl.when(jnp.logical_not((c == zh) & (zh == h)))(copy.wait_recv)
    own_tokens[...] = tokens([gvr[0], gvr[1]])

    def hidden_rows(i, carry):
        img, start = lax.div(i, 4), pl.multiple_of(lax.rem(i, 4) * 32, 32)
        flat = pl.multiple_of(i * 32, 32)
        grad_mod = mm(own_tokens[pl.ds(flat, 32), :], wrep[...])
        inv = stat_i[pl.ds(flat, 32), :]
        normal = (hid[img, pl.ds(start, 32), :].astype(F32) - stat_m[pl.ds(flat, 32), :]) * inv
        e = grad_mod * (1.0 + scalev[pl.ds(img, 1), :])
        mean_e = jnp.sum(e, axis=-1, keepdims=True) / D
        mean_n = jnp.sum(e * normal, axis=-1, keepdims=True) / D
        hgv[img, pl.ds(start, 32), :] = (inv * (e - mean_e - normal * mean_n)).astype(BF)
        return carry

    lax.fori_loop(0, 8, hidden_rows, 0)

    for copy in s1:
        copy.wait_recv()
    total = s1recv[0].astype(F32)
    for k in range(1, 16):
        total = total + s1recv[k].astype(F32)
    wt[0:48, :] = total
    for z in range(2):
        s2send[z] = wt[19 * z : 19 * z + 24, :]
    me_z = zl * 2 + zh

    def line_copy(n):
        dest_zl, dest_zh, dest_c = 2 * c + n // 4, (n // 2) % 2, n % 2
        copy = pltpu.make_async_remote_copy(
            src_ref=s2send.at[dest_zh], dst_ref=s2recv.at[me_z],
            send_sem=s2_s.at[n], recv_sem=s2_r.at[me_z],
            device_id={"batch": dest_zl * 4 + x, "tok": y * 2 + dest_zh, "grp": dest_c},
            device_id_type=MESH,
        )
        return copy, jnp.logical_not((dest_zl == zl) & (dest_zh == zh) & (dest_c == c))

    for n in range(8):
        copy, ok = line_copy(n)
        pl.when(ok)(copy.start)
    self_line = lax.div(zl, 2) == c

    @pl.when(self_line)
    def _():
        s2recv[me_z] = s2send[zh]

    for copy in pix_copies:
        copy.wait_recv()
    l384, k384 = iota((384, 384), 0), iota((384, 384), 1)
    cell = l384 & 127
    place = jnp.where(k384 == ((cell & 15) * 8 + (cell >> 4)) * 3 + (l384 >> 7), 1.0, 0.0)
    for i in range(2):
        slab = map_ref[i]
        block = pixg[i, slab >> 1]
        odd = jnp.full((24, 128), slab & 1, jnp.int32) == 1
        block = jnp.where(odd, pltpu.roll(block, 20, 0), block)
        wide = jnp.concatenate([block[0:8], block[8:16], block[16:24]], axis=1)
        moved = lax.dot_general(
            wide, place, (((1,), (0,)), ((), ())),
            precision=lax.Precision.HIGHEST, preferred_element_type=F32,
        )
        pix_out[i, 0] = moved[0:4]

    rew_copy.wait_recv()
    lane = iota((1, 128), 1)
    rew_out[...] = jnp.where(lane == 0, rewb[0, 0:1, :], rewb[1, 0:1, :])[:, 0:2]

    for n in range(8):
        copy = pltpu.make_async_remote_copy(
            src_ref=s2send.at[0], dst_ref=s2recv.at[n],
            send_sem=s2_s.at[0], recv_sem=s2_r.at[n],
            device_id={"grp": 1 - c}, device_id_type=MESH,
        )
        pl.when(jnp.logical_not(self_line & (me_z == n)))(copy.wait_recv)
    total = s2recv[0]
    for k in range(1, 8):
        total = total + s2recv[k]
    odd = jnp.full((24, 128), lax.rem(zl, 2), jnp.int32) == 1
    total = jnp.where(odd, pltpu.roll(total, 64, 1), total)
    wg_ref[...] = total[0:19, 0:64]

    for h in range(2):
        for copy, ok in lat_copies(h):
            pl.when(ok)(copy.wait_send)
    for copy in ex1 + ex2 + ex3 + pix_copies + s1 + mod_copies + [rew_copy, gv_pair]:
        copy.wait_send()
    for e in range(2):
        copy, ok = gv_copy(e)
        pl.when(ok)(copy.wait_send)
    for n in range(8):
        copy, ok = line_copy(n)
        pl.when(ok)(copy.wait_send)


def hand_out(*refs):
    sem = refs[8]
    pairs = [(refs[i], refs[4 + i]) for i in range(1, 4)]
    for h in range(2):
        for k in range(4):
            rows = pl.ds(k * 32, 32)
            pairs.append((refs[0].at[h, rows, :], refs[4].at[h, rows, :]))
    copies = [pltpu.make_async_copy(src, dst, sem.at[i]) for i, (src, dst) in enumerate(pairs)]
    for copy in copies:
        copy.start()
    for copy in copies:
        copy.wait()


def local(
    hidden, shift, scale, out_weight, noisy_latent, timestep, in_kernel, in_bias,
    norm_gain, norm_bias, mid_kernel, mid_bias, rgb_weight, clip_weight, text_embed, slab_map,
):
    any_spec = pl.BlockSpec(memory_space=pl.ANY)
    smem = pl.BlockSpec(memory_space=pltpu.SMEM)
    vmem = pl.BlockSpec(memory_space=pltpu.VMEM)
    dma = pltpu.SemaphoreType.DMA

    def v(dtype, *shape):
        return pltpu.VMEM(shape, dtype)

    hg, wg, reward, pixels = pl.pallas_call(
        kernel,
        out_shape=(
            pltpu.VMEM((2, 128, D), BF),
            pltpu.VMEM((19, 64), F32),
            pltpu.VMEM((1, 2), F32),
            pltpu.VMEM((2, 1, 4, 384), F32),
        ),
        in_specs=[smem, smem] + [any_spec] * 14,
        out_specs=(vmem, vmem, vmem, vmem),
        scratch_shapes=[
            v(BF, 2, 128, D), v(F32, 2, D), v(F32, 2, D), v(BF, 64, D), v(F32, 2, 4, 2048),
            v(BF, 3, 3, 16, CH), v(F32, 1, CH), v(F32, 1, CH), v(F32, 1, CH),
            v(BF, 3, 3, CH, CH), v(F32, 1, CH), v(BF, 3, CH), v(BF, CH, EMB), v(F32, 2, EMB),
            v(F32, 256, 1), v(F32, 256, 1), v(BF, 256, D), v(BF, 2, D, 128), v(BF, D // 2, 512),
            v(BF, 256, D), v(F32, 2, 256, 128), v(F32, 2, 4, 16, 128), v(BF, 2, 64, 128),
            v(BF, 4, 64, 128), v(BF, 224, 512), v(BF, 512, 8 * CH),
            v(F32, 14, 8, 16, CH), v(BF, 14, 10, 16, CH), v(F32, 12, 8, 16, CH),
            v(BF, 12, 10, 16, CH), v(F32, 10, 8, 16, CH), v(BF, 160, 8 * CH), v(F32, 8, 128),
            v(F32, 8, 8, 128), v(F32, 8, 8, 128), v(F32, 8, 8, 128), v(F32, 2, 8, 128),
            v(F32, 2, 8, 24, 128), v(BF, 2, 2, 64, 128), v(BF, 2, 64, 128), v(F32, 608, 128),
            v(BF, 16, 48, 128), v(BF, 16, 48, 128), v(F32, 2, 24, 128), v(F32, 8, 24, 128),
            v(BF, 256, 256),
            dma((14,)), dma((4,)), dma((4,)), dma((3, 7)), dma((3, 7)), dma((15,)), dma((15,)),
            dma, dma, dma((2, 3)), dma((2, 3)), dma, dma, dma((2,)), dma((2,)), dma((15,)), dma((15,)), dma((8,)), dma((8,)),
        ],
        compiler_params=pltpu.CompilerParams(
            collective_id=0, has_side_effects=True, vmem_limit_bytes=58 * 2**20
        ),
    )(
        timestep, slab_map.reshape(2), hidden, shift, scale, out_weight.T, noisy_latent, in_kernel,
        in_bias.reshape(1, CH), norm_gain.reshape(1, CH), norm_bias.reshape(1, CH),
        mid_kernel, mid_bias.reshape(1, CH), rgb_weight.T, clip_weight, text_embed,
    )
    hg, wg, reward, pixels = pl.pallas_call(
        hand_out,
        out_shape=(
            jax.ShapeDtypeStruct((2, 128, D), BF),
            jax.ShapeDtypeStruct((19, 64), F32),
            jax.ShapeDtypeStruct((1, 2), F32),
            jax.ShapeDtypeStruct((2, 1, 4, 384), F32),
        ),
        in_specs=[vmem] * 4,
        out_specs=[any_spec] * 4,
        scratch_shapes=[dma((11,))],
    )(*[pltpu.with_memory_space_constraint(out, pltpu.VMEM) for out in (hg, wg, reward, pixels)])
    return hg, wg, reward.reshape(2), pixels


def solution(mesh):
    rows = ("tok", "grp")
    return jax.shard_map(
        local,
        mesh=mesh,
        in_specs=(
            P("batch", rows, None), P("batch", None), P("batch", None), P(),
            P("batch", rows, None), P("batch"), P(), P(), P(), P(), P(), P(), P(), P(),
            P("batch", None), P("batch", rows),
        ),
        out_specs=(
            P("batch", rows, None), P(("batch", "tok"), None), P("batch"),
            P("batch", rows, None, None),
        ),
        check_vma=False,
    )
```

```python
import jax
import jax.numpy as jnp
from jax import lax
from jax.experimental import pallas as pl
from jax.experimental.pallas import tpu as pltpu
from jax.sharding import PartitionSpec as P

D = 2432
CH = 512
EMB = 1024
GROUP_N = 131072.0
CELLS = 8192.0
EPS = 1e-6
LSCALE = 1.5305
LSHIFT = 0.0609
REWARD_W = 16.0
BF = jnp.bfloat16
F32 = jnp.float32
MESH = pl.DeviceIdType.MESH

NT = (((1,), (1,)), ((), ()))


def mm(a, b):
    return jnp.dot(a, b, preferred_element_type=F32)


def mm_nt(a, b):
    return lax.dot_general(a, b, NT, preferred_element_type=F32)


def iota(shape, dim):
    return lax.broadcasted_iota(jnp.int32, shape, dim)


def one_hot(cond):
    return jnp.where(cond, 1.0, 0.0).astype(BF)


def noise_level(step, shape):
    fraction = (jnp.full(shape, step, jnp.int32).astype(F32) + 1.0) / 1000.0
    return 3.0 * fraction / (1.0 + 2.0 * fraction)


def group_total(tile):
    lane = iota(tile.shape, 1)
    for step in (1, 2, 4, 8):
        tile = tile + jnp.where(
            (lane & step) != 0, pltpu.roll(tile, step, 1), pltpu.roll(tile, 128 - step, 1)
        )
    return tile


def kernel(
    time_ref, map_ref,
    hidden_h, shift_h, scale_h, outw_h, noisy_h, ink_h, inb_h, gain_h, nbias_h,
    midk_h, midb_h, rgb_h, clip_h, text_h,
    hgv, wg_ref, rew_out, pix_out,
    hid, shiftv, scalev, outw, noisy, ink, inb, gain, nbias, midk, midb, rgb, clip, text,
    stat_m, stat_i, mod, modt, modp, wrep, ve, nl, latsend, rbuf, lhs, wb,
    first, act, slope, gsec, wgr, outer, rowbuf,
    p1, p2, p3, rewb, pixg, gvx, gvr, wt, s1send, s1recv, s2send, s2recv, own_tokens,
    load_sem, lat_s, lat_r, ex_s, ex_r, pix_s, pix_r, rew_s, rew_r, mod_s, mod_r,
    gx_s, gx_r, gv_s, gv_r, s1_s, s1_r, s2_s, s2_r,
):
    bt = lax.axis_index("batch")
    tok = lax.axis_index("tok")
    c = lax.axis_index("grp")
    y, zh = lax.div(tok, 2), lax.rem(tok, 2)
    zl, x = lax.div(bt, 4), lax.rem(bt, 4)
    j = 2 * y + c

    pairs = [
        (outw_h, outw), (scale_h, scalev), (shift_h, shiftv), (hidden_h, hid),
        (noisy_h, noisy), (ink_h, ink), (inb_h, inb), (gain_h, gain), (nbias_h, nbias),
        (midb_h, midb), (rgb_h, rgb), (midk_h, midk), (clip_h, clip), (text_h, text),
    ]
    loads = [
        pltpu.make_async_copy(src, dst, load_sem.at[i]) for i, (src, dst) in enumerate(pairs)
    ]
    for copy in loads[:4]:
        copy.start()

    bar = pltpu.get_barrier_semaphore()

    def greet(**where):
        pl.semaphore_signal(bar, inc=1, device_id=where, device_id_type=MESH)

    for d in range(15, 0, -1):
        n = lax.rem(tok * 2 + c + d, 16)
        greet(tok=lax.div(n, 2), grp=lax.rem(n, 2))
    for dz in range(1, 4):
        for n in range(4):
            greet(batch=lax.rem(zl + dz, 4) * 4 + x, tok=y * 2 + n // 2, grp=n % 2)
    for dx in range(1, 4):
        for dy in range(4):
            greet(batch=zl * 4 + lax.rem(x + dx, 4), tok=lax.rem(y + dy, 4) * 2 + zh)
    for copy in loads[4:]:
        copy.start()

    loads[0].wait()
    j256, k64 = iota((256, 64), 0), iota((256, 64), 1)
    spread = one_hot(((k64 >> 5) == (j256 >> 7)) & ((k64 & 31) == (j256 & 31)))
    wrep[...] = mm(spread, outw[...]).astype(BF)

    for copy in loads[1:4]:
        copy.wait()

    def norm_rows(i, carry):
        img, start = lax.div(i, 4), pl.multiple_of(lax.rem(i, 4) * 32, 32)
        flat = pl.multiple_of(i * 32, 32)
        values = hid[img, pl.ds(start, 32), :].astype(F32)
        mean = jnp.sum(values, axis=-1, keepdims=True) / D
        centered = values - mean
        inv = lax.rsqrt(jnp.sum(centered * centered, axis=-1, keepdims=True) / D + EPS)
        stat_m[pl.ds(flat, 32), :] = mean
        stat_i[pl.ds(flat, 32), :] = inv
        gain_row = 1.0 + scalev[pl.ds(img, 1), :]
        mod[pl.ds(flat, 32), :] = (
            centered * inv * gain_row + shiftv[pl.ds(img, 1), :]
        ).astype(BF)
        return carry

    lax.fori_loop(0, 8, norm_rows, 0)
    velocity = mm_nt(mod[...], wrep[...])
    for a in range(2):
        ve[a] = velocity[:, a * 128 : a * 128 + 128]

    loads[4].wait()
    for i in range(2):
        for b in range(16):
            nl[i, :, b, :] = noisy[i, :, b * 128 : (b + 1) * 128]
    lane_chi = iota((64, 128), 1) >> 5
    vel = [jnp.zeros((64, 128), F32)] * 2
    for chi in range(4):
        for a in range(2):
            vel[a] = jnp.where(lane_chi == chi, ve[a, pl.ds(chi, 64, stride=4), :], vel[a])
    for i in range(2):
        sigma = noise_level(time_ref[i], (16, 128))
        for p in range(2):
            for a in range(2):
                r = 2 * p + a
                part = vel[a][(i * 2 + p) * 16 : (i * 2 + p) * 16 + 16, :]
                latsend[i, r * 16 : r * 16 + 16, :] = (
                    (nl[i, r] - sigma * part) / LSCALE + LSHIFT
                ).astype(BF)

    pl.semaphore_wait(bar, 39)

    main_pos = 1 + c
    halo_j = 2 * y + zh + 2 * c - 1
    halo_pos = 3 - 3 * c
    halo_ok = (halo_j >= 0) & (halo_j <= 7)
    self_main = c == zh

    def lat_copies(h):
        here = zh == h
        main = pltpu.make_async_remote_copy(
            src_ref=latsend.at[h], dst_ref=rbuf.at[main_pos],
            send_sem=lat_s.at[2 * h], recv_sem=lat_r.at[main_pos],
            device_id={"tok": y * 2 + h, "grp": zh}, device_id_type=MESH,
        )
        halo = pltpu.make_async_remote_copy(
            src_ref=latsend.at[h], dst_ref=rbuf.at[halo_pos],
            send_sem=lat_s.at[2 * h + 1], recv_sem=lat_r.at[halo_pos],
            device_id={"tok": lax.div(halo_j, 2) * 2 + h, "grp": lax.rem(halo_j, 2)},
            device_id_type=MESH,
        )
        main_ok = jnp.logical_not(here & self_main)
        far_ok = halo_ok & jnp.logical_not(here & jnp.logical_not(self_main))
        return (main, main_ok), (halo, far_ok)

    for h in range(2):
        for copy, ok in lat_copies(h):
            pl.when(ok)(copy.start)
    self_pos = jnp.where(self_main, main_pos, halo_pos)
    rbuf[self_pos] = latsend[zh]

    @pl.when(j == 0)
    def _():
        rbuf[0] = jnp.zeros((64, 128), BF)

    @pl.when(j == 7)
    def _():
        rbuf[3] = jnp.zeros((64, 128), BF)

    def flip(k, carry):
        start = pl.multiple_of(k * 128, 128)
        for h in range(2):
            block = mod[h * 128 : h * 128 + 128, pl.ds(start, 128)]
            modt[h, pl.ds(start, 128), :] = block.astype(F32).T.astype(BF)
        return carry

    lax.fori_loop(0, 19, flip, 0)
    half = D // 2
    place4 = zh * 2 + c
    mod_lane = pl.ds(pl.multiple_of(place4 * 128, 128), 128)
    modp[:, mod_lane] = modt[zh, pl.ds(pl.multiple_of(c * half, 64), half), :]
    mod_copies = []
    for d in range(1, 4):
        n = lax.rem(place4 + d, 4)
        h, core = lax.div(n, 2), lax.rem(n, 2)
        for part, (low, size) in enumerate(((0, 608), (608, 608))):
            mod_copies.append(
                pltpu.make_async_remote_copy(
                    src_ref=modt.at[h, pl.ds(pl.multiple_of(core * half + low, 32), size), :],
                    dst_ref=modp.at[low : low + size, mod_lane],
                    send_sem=mod_s.at[part, d - 1], recv_sem=mod_r.at[part, d - 1],
                    device_id={"tok": y * 2 + h, "grp": core}, device_id_type=MESH,
                )
            )
    for copy in mod_copies:
        copy.start()

    for copy in loads[5:11]:
        copy.wait()

    def clear(i, carry):
        wb[pl.ds(pl.multiple_of(i * 16, 16), 16), :] = jnp.zeros((16, 8 * CH), BF)
        return carry

    lax.fori_loop(0, 32, clear, 0)
    for dy in range(3):
        for dx in range(3):
            tap = ink[dy, dx]
            for o in range(8):
                i = o + dx - 1
                row = 384 + 32 * dy if i < 0 else 384 + 32 * dy + 16 if i > 7 else dy * 128 + 16 * i
                wb[row : row + 16, o * CH : (o + 1) * CH] = tap
    rgbt = mm(one_hot(iota((8, 3), 0) == iota((8, 3), 1)), rgb[...]).astype(BF)

    def wait_lat(pos, ok):
        copy = pltpu.make_async_remote_copy(
            src_ref=latsend.at[0], dst_ref=rbuf.at[pos],
            send_sem=lat_s.at[0], recv_sem=lat_r.at[pos],
            device_id={"tok": tok, "grp": 1 - c}, device_id_type=MESH,
        )
        pl.when(ok & (self_pos != pos))(copy.wait_recv)

    wait_lat(0, j > 0)
    wait_lat(1, j >= 0)
    wait_lat(2, j >= 0)
    wait_lat(3, j < 7)

    lat = rbuf[...].reshape(256, 128)
    lat32 = lat.astype(F32)
    blk = iota((256, 128), 0) & 15
    lane = iota((256, 128), 1)
    after = jnp.where((lane < 16) & (blk < 15), pltpu.roll(lat32, 255, 0), 0.0)
    before = jnp.where((lane >= 112) & (blk > 0), pltpu.roll(lat32, 1, 0), 0.0)
    edge = after + before
    side = sum(
        pltpu.roll(edge, 16 + 32 * dy, 1)[16 * dy : 16 * dy + 224] for dy in range(3)
    )
    for dy in range(3):
        lhs[:, dy * 128 : dy * 128 + 128] = lat[16 * dy : 16 * dy + 224]
    lhs[:, 384:512] = side.astype(BF)

    sum_one = jnp.zeros((8, CH), F32)
    sum_two = jnp.zeros((8, CH), F32)
    for o in range(8):
        out = mm(lhs[48:176, :], wb[:, o * CH : (o + 1) * CH]) + inb[...]
        first[3:11, o] = out.reshape(8, 16, CH)
        own = out.reshape(16, 8, CH)
        sum_one = sum_one + jnp.sum(own, axis=0)
        sum_two = sum_two + jnp.sum(own * own, axis=0)

    def pack(buf, rows):
        for n, row in enumerate(rows):
            row = jnp.sum(row, axis=0, keepdims=True)
            for k in range(4):
                buf[j, n * 4 + k : n * 4 + k + 1, :] = row[:, k * 128 : k * 128 + 128]

    def exchange(phase, buf):
        copies = []
        offsets = ((2, 0), (2, 1), (1, 0), (3, 0), (1, 1), (3, 1), (0, 1))
        for d, (dy, dc) in enumerate(offsets):
            copies.append(
                pltpu.make_async_remote_copy(
                    src_ref=buf.at[j], dst_ref=buf.at[j],
                    send_sem=ex_s.at[phase, d], recv_sem=ex_r.at[phase, d],
                    device_id={"tok": lax.rem(y + dy, 4) * 2 + zh, "grp": lax.rem(c + dc, 2)},
                    device_id_type=MESH,
                )
            )
        for copy in copies:
            copy.start()
        return copies

    def collect(buf, copies):
        for copy in copies:
            copy.wait_recv()
        total = buf[0]
        for k in range(1, 8):
            total = total + buf[k]
        return total

    def as_row(tile, start):
        rowbuf[...] = tile
        return jnp.concatenate([rowbuf[start + k : start + k + 1, :] for k in range(4)], axis=1)

    pack(p1, (sum_one, sum_two))
    ex1 = exchange(0, p1)
    beside = jnp.concatenate([lhs[0:48, :], lhs[176:224, :]], axis=0)
    for o in range(8):
        out = (mm(beside, wb[:, o * CH : (o + 1) * CH]) + inb[...]).reshape(6, 16, CH)
        first[0:3, o] = out[0:3]
        first[11:14, o] = out[3:6]

    stats = group_total(collect(p1, ex1)) / GROUP_N
    mu = as_row(stats, 0)
    rstd = lax.rsqrt(as_row(stats, 4) - mu * mu + EPS)
    coef_a = rstd * gain[...] * 0.5
    coef_b = (nbias[...] - mu * rstd * gain[...]) * 0.5

    blk16 = iota((16, CH), 0)

    def put_row(buf, r, value):
        buf[r, 1:9] = value.astype(BF)
        buf[r, 0] = jnp.where(blk16 > 0, pltpu.roll(value[7], 1, 0), 0.0).astype(BF)
        buf[r, 9] = jnp.where(blk16 < 15, pltpu.roll(value[0], 15, 0), 0.0).astype(BF)

    def inside(row):
        return ((row >= 0) & (row < 64)).astype(F32)

    def act_rows(rows):
        for r in rows:
            half_u = first[r] * coef_a + coef_b
            put_row(act, r, half_u * (1.0 + jnp.tanh(half_u)) * inside(8 * j - 3 + r))

    act_rows((2, 3, 4, 5))

    loads[11].wait()

    def decode(pieces):
        total = None
        for dy in range(3):
            for dx in range(3):
                part = [act[r + dy : r + dy + n, dx : dx + 8].reshape(n * 128, CH) for r, n in pieces]
                part = part[0] if len(part) == 1 else jnp.concatenate(part, axis=0)
                term = mm(part, midk[dy, dx])
                total = term if total is None else total + term
        half_u = (total + midb[...]) * 0.5
        tanh = jnp.tanh(half_u)
        grad = 0.5 * ((1.0 + tanh) + half_u * (1.0 - tanh * tanh))
        return half_u * (1.0 + tanh), grad

    pooled_sum = jnp.zeros((8, CH), F32)
    for i in range(4):
        r = 2 + 2 * i
        act_rows(((6, 7), (8, 9), (10, 11), (0, 1, 12, 13))[i])
        value, grad = decode([(r, 2)])
        slope[r : r + 2] = grad.reshape(2, 8, 16, CH)
        pixel = mm_nt(rgbt, value.astype(BF))
        for colour in range(3):
            for row in range(2):
                at = colour * 8 + 2 * i + row
                pixg[zh, j, at : at + 1, :] = pixel[colour : colour + 1, row * 128 : row * 128 + 128]
        pooled_sum = pooled_sum + jnp.sum(value.reshape(32, 8, CH), axis=0)

    pack(p2, (pooled_sum,))
    ex2 = exchange(1, p2)

    pix_copies = []
    for d in range(1, 16):
        n = lax.rem(tok * 2 + c + d, 16)
        pix_copies.append(
            pltpu.make_async_remote_copy(
                src_ref=pixg.at[zh, j], dst_ref=pixg.at[zh, j],
                send_sem=pix_s.at[d - 1], recv_sem=pix_r.at[d - 1],
                device_id={"tok": lax.div(n, 2), "grp": lax.rem(n, 2)}, device_id_type=MESH,
            )
        )

    for r in range(10):
        half_u = first[r + 2] * coef_a + coef_b
        tanh = jnp.tanh(half_u)
        outer[r] = ((1.0 + tanh) + half_u * (1.0 - tanh * tanh)) * (gain[...] * 0.5)
    _, grad = decode([(0, 2), (10, 2)])
    slope[0:2] = grad[:256].reshape(2, 8, 16, CH)
    slope[10:12] = grad[256:].reshape(2, 8, 16, CH)

    loads[12].wait()
    loads[13].wait()
    pooled = (as_row(collect(p2, ex2), 0) / CELLS).astype(BF)
    for copy in pix_copies:
        copy.start()
    feature = mm(jnp.broadcast_to(pooled, (8, CH)), clip[...])
    target = text[pl.ds(zh, 1), :]
    norm_f = jnp.sqrt(jnp.sum(feature * feature, axis=-1, keepdims=True) + EPS)
    norm_t = jnp.sqrt(jnp.sum(target * target, axis=-1, keepdims=True) + EPS)
    reward = jnp.sum(feature * target, axis=-1, keepdims=True) / (norm_f * norm_t)
    grad_feature = (
        REWARD_W * (target / (norm_f * norm_t) - reward * feature / (norm_f * norm_f))
    ).astype(BF)
    grad_act = mm_nt(grad_feature, clip[...])[0:1, :]
    rewb[zh] = jnp.broadcast_to(reward, (8, 128))
    rew_copy = pltpu.make_async_remote_copy(
        src_ref=rewb.at[zh], dst_ref=rewb.at[zh], send_sem=rew_s, recv_sem=rew_r,
        device_id={"tok": y * 2 + 1 - zh}, device_id_type=MESH,
    )
    rew_copy.start()

    def grad_rows(rows):
        for r in rows:
            put_row(gsec, r, slope[r] * grad_act * inside(8 * j - 2 + r))

    grad_rows((1, 2, 3, 4))

    xh_b = mu * rstd

    def back(pieces):
        total = None
        for dy in range(3):
            for dx in range(3):
                part = [
                    gsec[r + 2 - dy : r + 2 - dy + n, 2 - dx : 10 - dx].reshape(n * 128, CH)
                    for r, n in pieces
                ]
                part = part[0] if len(part) == 1 else jnp.concatenate(part, axis=0)
                term = mm_nt(part, midk[dy, dx])
                total = term if total is None else total + term
        def rows_of(buf, shift):
            part = [buf[r + shift : r + shift + n].reshape(n * 128, CH) for r, n in pieces]
            return part[0] if len(part) == 1 else jnp.concatenate(part, axis=0)

        return total * rows_of(outer, 0), rows_of(first, 2) * rstd - xh_b

    sums = [jnp.zeros((8, CH), F32)] * 2
    for i in range(4):
        r = 1 + 2 * i
        grad_rows(((5, 6), (7, 8), (9, 10), (0, 11))[i])
        w, xhat = back([(r, 2)])
        wgr[r : r + 2] = w.reshape(2, 8, 16, CH)
        sums[0] = sums[0] + jnp.sum(w.reshape(32, 8, CH), axis=0)
        sums[1] = sums[1] + jnp.sum((w * xhat).reshape(32, 8, CH), axis=0)
    pack(p3, sums)
    ex3 = exchange(2, p3)
    w, _ = back([(0, 1), (9, 1)])
    wgr[0:1] = w[:128].reshape(1, 8, 16, CH)
    wgr[9:10] = w[128:].reshape(1, 8, 16, CH)

    stats = group_total(collect(p3, ex3)) / GROUP_N
    mean_w = as_row(stats, 0)
    mean_x = as_row(stats, 4)
    coef_f = -rstd * rstd * mean_x
    coef_0 = (xh_b * mean_x - mean_w) * rstd

    row = 8 * j - 1 + (iota((160, 1), 0) >> 4)
    keep_row = ((row >= 0) & (row < 64)).astype(F32)
    back_y = None
    for o in range(8):
        value = wgr[:, o].reshape(160, CH) * rstd + first[2:12, o].reshape(160, CH) * coef_f
        value = ((value + coef_0) * keep_row).astype(BF)
        term = mm_nt(value, wb[:, o * CH : (o + 1) * CH])
        back_y = term if back_y is None else back_y + term
    grad_lat = jnp.zeros((128, 128), F32)
    edge = jnp.zeros((128, 128), F32)
    lane = iota((128, 128), 1)
    blk = iota((128, 128), 0) & 15
    for dy in range(3):
        start = (2 - dy) * 16
        grad_lat = grad_lat + back_y[start : start + 128, dy * 128 : dy * 128 + 128]
        part = back_y[start : start + 128, 384:512]
        part = jnp.where((lane >> 5) == dy, part, 0.0)
        edge = edge + pltpu.roll(part, (112 - 32 * dy) % 128, 1)
    grad_lat = grad_lat + jnp.where((lane >= 112) & (blk < 15), pltpu.roll(edge, 127, 0), 0.0)
    grad_lat = grad_lat + jnp.where((lane < 16) & (blk > 0), pltpu.roll(edge, 1, 0), 0.0)
    sigma = noise_level(time_ref[zh], (128, 128))
    gvx[c] = (-sigma * (grad_lat / LSCALE)).astype(BF).reshape(2, 64, 128)

    gv_pair = pltpu.make_async_remote_copy(
        src_ref=gvx.at[c], dst_ref=gvx.at[c], send_sem=gx_s, recv_sem=gx_r,
        device_id={"grp": 1 - c}, device_id_type=MESH,
    )
    gv_pair.start()

    def gv_copy(e):
        copy = pltpu.make_async_remote_copy(
            src_ref=gvx.at[c, e], dst_ref=gvr.at[zh],
            send_sem=gv_s.at[e], recv_sem=gv_r.at[zh],
            device_id={"tok": y * 2 + c, "grp": e}, device_id_type=MESH,
        )
        return copy, jnp.logical_not((c == zh) & (c == e))

    for e in range(2):
        copy, ok = gv_copy(e)
        pl.when(ok)(copy.start)

    @pl.when(c == zh)
    def _():
        gvr[zh] = gvx[c, c]

    def tokens(parts):
        for a in range(2):
            rows = [
                part[(2 * p + a) * 16 : (2 * p + a) * 16 + 16, :] for part in parts for p in range(2)
            ]
            full = jnp.concatenate(rows, axis=0).astype(F32)
            for chi in range(4):
                ve[a, pl.ds(chi, 64, stride=4), :] = jnp.where(lane_chi == chi, full, 0.0)
        return jnp.concatenate([ve[0], ve[1]], axis=1).astype(BF)

    j_r, k_c = iota((256, 256), 0), iota((256, 256), 1)
    target_lane = j_r & 63
    keep = ((target_lane >> 5) == (k_c >> 7)) & ((target_lane & 31) == (k_c & 31))
    quad = one_hot(keep & ((j_r < 64) | (j_r >= 192)))
    for copy in mod_copies:
        copy.wait_recv()

    def term_of(row):
        grads = mm_nt(tokens([gvx[row, 0], gvx[row, 1]]), quad).astype(BF)
        lanes = pl.ds(pl.multiple_of(row * 256, 256), 256)
        return mm(modp[0:608, lanes], grads[:, :128]) + mm(modp[608:1216, lanes], grads[:, 128:])

    wt[...] = term_of(c) * (1.0 / 2048.0)
    gv_pair.wait_recv()
    wt[...] += term_of(1 - c) * (1.0 / 2048.0)
    for k in range(16):
        s1send[k, 0:32, :] = wt[38 * k : 38 * k + 32, :].astype(BF)
        tail = jnp.concatenate([wt[38 * k + 32 : 38 * k + 38, :], jnp.zeros((10, 128), F32)], axis=0)
        s1send[k, 32:48, :] = tail.astype(BF)
    me_xy = x * 4 + y
    s1 = []
    offsets = [(dx, dy) for dx in range(4) for dy in range(4) if dx or dy]
    offsets.sort(key=lambda o: -min(o[0], 4 - o[0]) - min(o[1], 4 - o[1]))
    for d, (dx, dy) in enumerate(offsets):
        to_x, to_y = lax.rem(x + dx, 4), lax.rem(y + dy, 4)
        s1.append(
            pltpu.make_async_remote_copy(
                src_ref=s1send.at[to_x * 4 + to_y], dst_ref=s1recv.at[me_xy],
                send_sem=s1_s.at[d], recv_sem=s1_r.at[d],
                device_id={"batch": zl * 4 + to_x, "tok": to_y * 2 + zh}, device_id_type=MESH,
            )
        )
    for copy in s1:
        copy.start()
    s1recv[me_xy] = s1send[me_xy]

    for h in range(2):
        copy = pltpu.make_async_remote_copy(
            src_ref=gvx.at[0, 0], dst_ref=gvr.at[h],
            send_sem=gv_s.at[0], recv_sem=gv_r.at[h],
            device_id={"tok": y * 2 + c, "grp": 0}, device_id_type=MESH,
        )
        pl.when(jnp.logical_not((c == zh) & (zh == h)))(copy.wait_recv)
    own_tokens[...] = tokens([gvr[0], gvr[1]])

    def hidden_rows(i, carry):
        img, start = lax.div(i, 4), pl.multiple_of(lax.rem(i, 4) * 32, 32)
        flat = pl.multiple_of(i * 32, 32)
        grad_mod = mm(own_tokens[pl.ds(flat, 32), :], wrep[...])
        inv = stat_i[pl.ds(flat, 32), :]
        normal = (hid[img, pl.ds(start, 32), :].astype(F32) - stat_m[pl.ds(flat, 32), :]) * inv
        e = grad_mod * (1.0 + scalev[pl.ds(img, 1), :])
        mean_e = jnp.sum(e, axis=-1, keepdims=True) / D
        mean_n = jnp.sum(e * normal, axis=-1, keepdims=True) / D
        hgv[img, pl.ds(start, 32), :] = (inv * (e - mean_e - normal * mean_n)).astype(BF)
        return carry

    lax.fori_loop(0, 8, hidden_rows, 0)

    for copy in s1:
        copy.wait_recv()
    total = s1recv[0].astype(F32)
    for k in range(1, 16):
        total = total + s1recv[k].astype(F32)
    wt[0:48, :] = total
    for z in range(2):
        s2send[z] = wt[19 * z : 19 * z + 24, :]
    me_z = zl * 2 + zh

    def line_copy(n):
        dest_zl, dest_zh, dest_c = 2 * c + n // 4, (n // 2) % 2, n % 2
        copy = pltpu.make_async_remote_copy(
            src_ref=s2send.at[dest_zh], dst_ref=s2recv.at[me_z],
            send_sem=s2_s.at[n], recv_sem=s2_r.at[me_z],
            device_id={"batch": dest_zl * 4 + x, "tok": y * 2 + dest_zh, "grp": dest_c},
            device_id_type=MESH,
        )
        return copy, jnp.logical_not((dest_zl == zl) & (dest_zh == zh) & (dest_c == c))

    for n in range(8):
        copy, ok = line_copy(n)
        pl.when(ok)(copy.start)
    self_line = lax.div(zl, 2) == c

    @pl.when(self_line)
    def _():
        s2recv[me_z] = s2send[zh]

    for copy in pix_copies:
        copy.wait_recv()
    l384, k384 = iota((384, 384), 0), iota((384, 384), 1)
    cell = l384 & 127
    place = jnp.where(k384 == ((cell & 15) * 8 + (cell >> 4)) * 3 + (l384 >> 7), 1.0, 0.0)
    for i in range(2):
        slab = map_ref[i]
        block = pixg[i, slab >> 1]
        odd = jnp.full((24, 128), slab & 1, jnp.int32) == 1
        block = jnp.where(odd, pltpu.roll(block, 20, 0), block)
        wide = jnp.concatenate([block[0:8], block[8:16], block[16:24]], axis=1)
        moved = lax.dot_general(
            wide, place, (((1,), (0,)), ((), ())),
            precision=lax.Precision.HIGHEST, preferred_element_type=F32,
        )
        pix_out[i, 0] = moved[0:4]

    rew_copy.wait_recv()
    lane = iota((1, 128), 1)
    rew_out[...] = jnp.where(lane == 0, rewb[0, 0:1, :], rewb[1, 0:1, :])[:, 0:2]

    for n in range(8):
        copy = pltpu.make_async_remote_copy(
            src_ref=s2send.at[0], dst_ref=s2recv.at[n],
            send_sem=s2_s.at[0], recv_sem=s2_r.at[n],
            device_id={"grp": 1 - c}, device_id_type=MESH,
        )
        pl.when(jnp.logical_not(self_line & (me_z == n)))(copy.wait_recv)
    total = s2recv[0]
    for k in range(1, 8):
        total = total + s2recv[k]
    odd = jnp.full((24, 128), lax.rem(zl, 2), jnp.int32) == 1
    total = jnp.where(odd, pltpu.roll(total, 64, 1), total)
    wg_ref[...] = total[0:19, 0:64]

    for h in range(2):
        for copy, ok in lat_copies(h):
            pl.when(ok)(copy.wait_send)
    for copy in ex1 + ex2 + ex3 + pix_copies + s1 + mod_copies + [rew_copy, gv_pair]:
        copy.wait_send()
    for e in range(2):
        copy, ok = gv_copy(e)
        pl.when(ok)(copy.wait_send)
    for n in range(8):
        copy, ok = line_copy(n)
        pl.when(ok)(copy.wait_send)


def hand_out(*refs):
    sem = refs[8]
    pairs = [(refs[i], refs[4 + i]) for i in range(1, 4)]
    for h in range(2):
        for k in range(4):
            rows = pl.ds(k * 32, 32)
            pairs.append((refs[0].at[h, rows, :], refs[4].at[h, rows, :]))
    copies = [pltpu.make_async_copy(src, dst, sem.at[i]) for i, (src, dst) in enumerate(pairs)]
    for copy in copies:
        copy.start()
    for copy in copies:
        copy.wait()


def local(
    hidden, shift, scale, out_weight, noisy_latent, timestep, in_kernel, in_bias,
    norm_gain, norm_bias, mid_kernel, mid_bias, rgb_weight, clip_weight, text_embed, slab_map,
):
    any_spec = pl.BlockSpec(memory_space=pl.ANY)
    smem = pl.BlockSpec(memory_space=pltpu.SMEM)
    vmem = pl.BlockSpec(memory_space=pltpu.VMEM)
    dma = pltpu.SemaphoreType.DMA

    def v(dtype, *shape):
        return pltpu.VMEM(shape, dtype)

    hg, wg, reward, pixels = pl.pallas_call(
        kernel,
        out_shape=(
            pltpu.VMEM((2, 128, D), BF),
            pltpu.VMEM((19, 64), F32),
            pltpu.VMEM((1, 2), F32),
            pltpu.VMEM((2, 1, 4, 384), F32),
        ),
        in_specs=[smem, smem] + [any_spec] * 14,
        out_specs=(vmem, vmem, vmem, vmem),
        scratch_shapes=[
            v(BF, 2, 128, D), v(F32, 2, D), v(F32, 2, D), v(BF, 64, D), v(F32, 2, 4, 2048),
            v(BF, 3, 3, 16, CH), v(F32, 1, CH), v(F32, 1, CH), v(F32, 1, CH),
            v(BF, 3, 3, CH, CH), v(F32, 1, CH), v(BF, 3, CH), v(BF, CH, EMB), v(F32, 2, EMB),
            v(F32, 256, 1), v(F32, 256, 1), v(BF, 256, D), v(BF, 2, D, 128), v(BF, D // 2, 512),
            v(BF, 256, D), v(F32, 2, 256, 128), v(F32, 2, 4, 16, 128), v(BF, 2, 64, 128),
            v(BF, 4, 64, 128), v(BF, 224, 512), v(BF, 512, 8 * CH),
            v(F32, 14, 8, 16, CH), v(BF, 14, 10, 16, CH), v(F32, 12, 8, 16, CH),
            v(BF, 12, 10, 16, CH), v(F32, 10, 8, 16, CH), v(F32, 10, 8, 16, CH), v(F32, 8, 128),
            v(F32, 8, 8, 128), v(F32, 8, 8, 128), v(F32, 8, 8, 128), v(F32, 2, 8, 128),
            v(F32, 2, 8, 24, 128), v(BF, 2, 2, 64, 128), v(BF, 2, 64, 128), v(F32, 608, 128),
            v(BF, 16, 48, 128), v(BF, 16, 48, 128), v(F32, 2, 24, 128), v(F32, 8, 24, 128),
            v(BF, 256, 256),
            dma((14,)), dma((4,)), dma((4,)), dma((3, 7)), dma((3, 7)), dma((15,)), dma((15,)),
            dma, dma, dma((2, 3)), dma((2, 3)), dma, dma, dma((2,)), dma((2,)), dma((15,)), dma((15,)), dma((8,)), dma((8,)),
        ],
        compiler_params=pltpu.CompilerParams(
            collective_id=0, has_side_effects=True, vmem_limit_bytes=58 * 2**20
        ),
    )(
        timestep, slab_map.reshape(2), hidden, shift, scale, out_weight.T, noisy_latent, in_kernel,
        in_bias.reshape(1, CH), norm_gain.reshape(1, CH), norm_bias.reshape(1, CH),
        mid_kernel, mid_bias.reshape(1, CH), rgb_weight.T, clip_weight, text_embed,
    )
    hg, wg, reward, pixels = pl.pallas_call(
        hand_out,
        out_shape=(
            jax.ShapeDtypeStruct((2, 128, D), BF),
            jax.ShapeDtypeStruct((19, 64), F32),
            jax.ShapeDtypeStruct((1, 2), F32),
            jax.ShapeDtypeStruct((2, 1, 4, 384), F32),
        ),
        in_specs=[vmem] * 4,
        out_specs=[any_spec] * 4,
        scratch_shapes=[dma((11,))],
    )(*[pltpu.with_memory_space_constraint(out, pltpu.VMEM) for out in (hg, wg, reward, pixels)])
    return hg, wg, reward.reshape(2), pixels


def solution(mesh):
    rows = ("tok", "grp")
    return jax.shard_map(
        local,
        mesh=mesh,
        in_specs=(
            P("batch", rows, None), P("batch", None), P("batch", None), P(),
            P("batch", rows, None), P("batch"), P(), P(), P(), P(), P(), P(), P(), P(),
            P("batch", None), P("batch", rows),
        ),
        out_specs=(
            P("batch", rows, None), P(("batch", "tok"), None), P("batch"),
            P("batch", rows, None, None),
        ),
        check_vma=False,
    )
```

```python
import jax
import jax.numpy as jnp
from jax import lax
from jax.experimental import pallas as pl
from jax.experimental.pallas import tpu as pltpu
from jax.sharding import PartitionSpec as P

D = 2432
CH = 512
EMB = 1024
GROUP_N = 131072.0
CELLS = 8192.0
EPS = 1e-6
LSCALE = 1.5305
LSHIFT = 0.0609
REWARD_W = 16.0
BF = jnp.bfloat16
F32 = jnp.float32
MESH = pl.DeviceIdType.MESH

NT = (((1,), (1,)), ((), ()))


def mm(a, b):
    return jnp.dot(a, b, preferred_element_type=F32)


def mm_nt(a, b):
    return lax.dot_general(a, b, NT, preferred_element_type=F32)


def iota(shape, dim):
    return lax.broadcasted_iota(jnp.int32, shape, dim)


def one_hot(cond):
    return jnp.where(cond, 1.0, 0.0).astype(BF)


def noise_level(step, shape):
    fraction = (jnp.full(shape, step, jnp.int32).astype(F32) + 1.0) / 1000.0
    return 3.0 * fraction / (1.0 + 2.0 * fraction)


def group_total(tile):
    lane = iota(tile.shape, 1)
    for step in (1, 2, 4, 8):
        tile = tile + jnp.where(
            (lane & step) != 0, pltpu.roll(tile, step, 1), pltpu.roll(tile, 128 - step, 1)
        )
    return tile


def kernel(
    time_ref, map_ref,
    hidden_h, shift_h, scale_h, outw_h, noisy_h, ink_h, inb_h, gain_h, nbias_h,
    midk_h, midb_h, rgb_h, clip_h, text_h,
    hgv, wg_ref, rew_out, pix_out,
    hid, shiftv, scalev, outw, noisy, ink, inb, gain, nbias, midk, midb, rgb, clip, text,
    stat_m, stat_i, mod, modt, modp, wrep, ve, nl, latsend, rbuf, lhs, wb,
    first, act, slope, gsec, wgr, outer, rowbuf,
    p1, p2, p3, rewb, pixg, gvx, gvr, wt, s1send, s1recv, s2send, s2recv, own_tokens,
    load_sem, lat_s, lat_r, ex_s, ex_r, pix_s, pix_r, rew_s, rew_r, mod_s, mod_r,
    gx_s, gx_r, gv_s, gv_r, s1_s, s1_r, s2_s, s2_r,
):
    bt = lax.axis_index("batch")
    tok = lax.axis_index("tok")
    c = lax.axis_index("grp")
    y, zh = lax.div(tok, 2), lax.rem(tok, 2)
    zl, x = lax.div(bt, 4), lax.rem(bt, 4)
    j = 2 * y + c

    pairs = [
        (outw_h, outw), (scale_h, scalev), (shift_h, shiftv), (hidden_h, hid),
        (noisy_h, noisy), (ink_h, ink), (inb_h, inb), (gain_h, gain), (nbias_h, nbias),
        (midb_h, midb), (rgb_h, rgb), (midk_h, midk), (clip_h, clip), (text_h, text),
    ]
    loads = [
        pltpu.make_async_copy(src, dst, load_sem.at[i]) for i, (src, dst) in enumerate(pairs)
    ]
    for copy in loads[:4]:
        copy.start()

    bar = pltpu.get_barrier_semaphore()

    def greet(**where):
        pl.semaphore_signal(bar, inc=1, device_id=where, device_id_type=MESH)

    for d in range(15, 0, -1):
        n = lax.rem(tok * 2 + c + d, 16)
        greet(tok=lax.div(n, 2), grp=lax.rem(n, 2))
    for dz in range(1, 4):
        for n in range(4):
            greet(batch=lax.rem(zl + dz, 4) * 4 + x, tok=y * 2 + n // 2, grp=n % 2)
    for dx in range(1, 4):
        for dy in range(4):
            greet(batch=zl * 4 + lax.rem(x + dx, 4), tok=lax.rem(y + dy, 4) * 2 + zh)
    for copy in loads[4:]:
        copy.start()

    loads[0].wait()
    j256, k64 = iota((256, 64), 0), iota((256, 64), 1)
    spread = one_hot(((k64 >> 5) == (j256 >> 7)) & ((k64 & 31) == (j256 & 31)))
    wrep[...] = mm(spread, outw[...]).astype(BF)

    for copy in loads[1:4]:
        copy.wait()

    def norm_rows(i, carry):
        img, start = lax.div(i, 4), pl.multiple_of(lax.rem(i, 4) * 32, 32)
        flat = pl.multiple_of(i * 32, 32)
        values = hid[img, pl.ds(start, 32), :].astype(F32)
        mean = jnp.sum(values, axis=-1, keepdims=True) / D
        centered = values - mean
        inv = lax.rsqrt(jnp.sum(centered * centered, axis=-1, keepdims=True) / D + EPS)
        stat_m[pl.ds(flat, 32), :] = mean
        stat_i[pl.ds(flat, 32), :] = inv
        gain_row = 1.0 + scalev[pl.ds(img, 1), :]
        mod[pl.ds(flat, 32), :] = (
            centered * inv * gain_row + shiftv[pl.ds(img, 1), :]
        ).astype(BF)
        return carry

    lax.fori_loop(0, 8, norm_rows, 0)
    velocity = mm_nt(mod[...], wrep[...])
    for a in range(2):
        ve[a] = velocity[:, a * 128 : a * 128 + 128]

    loads[4].wait()
    for i in range(2):
        for b in range(16):
            nl[i, :, b, :] = noisy[i, :, b * 128 : (b + 1) * 128]
    lane_chi = iota((64, 128), 1) >> 5
    vel = [jnp.zeros((64, 128), F32)] * 2
    for chi in range(4):
        for a in range(2):
            vel[a] = jnp.where(lane_chi == chi, ve[a, pl.ds(chi, 64, stride=4), :], vel[a])
    for i in range(2):
        sigma = noise_level(time_ref[i], (16, 128))
        for p in range(2):
            for a in range(2):
                r = 2 * p + a
                part = vel[a][(i * 2 + p) * 16 : (i * 2 + p) * 16 + 16, :]
                latsend[i, r * 16 : r * 16 + 16, :] = (
                    (nl[i, r] - sigma * part) / LSCALE + LSHIFT
                ).astype(BF)

    pl.semaphore_wait(bar, 39)

    main_pos = 1 + c
    halo_j = 2 * y + zh + 2 * c - 1
    halo_pos = 3 - 3 * c
    halo_ok = (halo_j >= 0) & (halo_j <= 7)
    self_main = c == zh

    def lat_copies(h):
        here = zh == h
        main = pltpu.make_async_remote_copy(
            src_ref=latsend.at[h], dst_ref=rbuf.at[main_pos],
            send_sem=lat_s.at[2 * h], recv_sem=lat_r.at[main_pos],
            device_id={"tok": y * 2 + h, "grp": zh}, device_id_type=MESH,
        )
        halo = pltpu.make_async_remote_copy(
            src_ref=latsend.at[h], dst_ref=rbuf.at[halo_pos],
            send_sem=lat_s.at[2 * h + 1], recv_sem=lat_r.at[halo_pos],
            device_id={"tok": lax.div(halo_j, 2) * 2 + h, "grp": lax.rem(halo_j, 2)},
            device_id_type=MESH,
        )
        main_ok = jnp.logical_not(here & self_main)
        far_ok = halo_ok & jnp.logical_not(here & jnp.logical_not(self_main))
        return (main, main_ok), (halo, far_ok)

    for h in range(2):
        for copy, ok in lat_copies(h):
            pl.when(ok)(copy.start)
    self_pos = jnp.where(self_main, main_pos, halo_pos)
    rbuf[self_pos] = latsend[zh]

    @pl.when(j == 0)
    def _():
        rbuf[0] = jnp.zeros((64, 128), BF)

    @pl.when(j == 7)
    def _():
        rbuf[3] = jnp.zeros((64, 128), BF)

    def flip(k, carry):
        start = pl.multiple_of(k * 128, 128)
        for h in range(2):
            block = mod[h * 128 : h * 128 + 128, pl.ds(start, 128)]
            modt[h, pl.ds(start, 128), :] = block.astype(F32).T.astype(BF)
        return carry

    lax.fori_loop(0, 19, flip, 0)
    half = D // 2
    place4 = zh * 2 + c
    mod_lane = pl.ds(pl.multiple_of(place4 * 128, 128), 128)
    modp[:, mod_lane] = modt[zh, pl.ds(pl.multiple_of(c * half, 64), half), :]
    mod_copies = []
    for d in range(1, 4):
        n = lax.rem(place4 + d, 4)
        h, core = lax.div(n, 2), lax.rem(n, 2)
        for part, (low, size) in enumerate(((0, 608), (608, 608))):
            mod_copies.append(
                pltpu.make_async_remote_copy(
                    src_ref=modt.at[h, pl.ds(pl.multiple_of(core * half + low, 32), size), :],
                    dst_ref=modp.at[low : low + size, mod_lane],
                    send_sem=mod_s.at[part, d - 1], recv_sem=mod_r.at[part, d - 1],
                    device_id={"tok": y * 2 + h, "grp": core}, device_id_type=MESH,
                )
            )
    for copy in mod_copies:
        copy.start()

    for copy in loads[5:11]:
        copy.wait()

    def clear(i, carry):
        wb[pl.ds(pl.multiple_of(i * 16, 16), 16), :] = jnp.zeros((16, 8 * CH), BF)
        return carry

    lax.fori_loop(0, 32, clear, 0)
    for dy in range(3):
        for dx in range(3):
            tap = ink[dy, dx]
            for o in range(8):
                i = o + dx - 1
                row = 384 + 32 * dy if i < 0 else 384 + 32 * dy + 16 if i > 7 else dy * 128 + 16 * i
                wb[row : row + 16, o * CH : (o + 1) * CH] = tap
    rgbt = mm(one_hot(iota((8, 3), 0) == iota((8, 3), 1)), rgb[...]).astype(BF)

    def wait_lat(pos, ok):
        copy = pltpu.make_async_remote_copy(
            src_ref=latsend.at[0], dst_ref=rbuf.at[pos],
            send_sem=lat_s.at[0], recv_sem=lat_r.at[pos],
            device_id={"tok": tok, "grp": 1 - c}, device_id_type=MESH,
        )
        pl.when(ok & (self_pos != pos))(copy.wait_recv)

    wait_lat(0, j > 0)
    wait_lat(1, j >= 0)
    wait_lat(2, j >= 0)
    wait_lat(3, j < 7)

    lat = rbuf[...].reshape(256, 128)
    lat32 = lat.astype(F32)
    blk = iota((256, 128), 0) & 15
    lane = iota((256, 128), 1)
    after = jnp.where((lane < 16) & (blk < 15), pltpu.roll(lat32, 255, 0), 0.0)
    before = jnp.where((lane >= 112) & (blk > 0), pltpu.roll(lat32, 1, 0), 0.0)
    edge = after + before
    side = sum(
        pltpu.roll(edge, 16 + 32 * dy, 1)[16 * dy : 16 * dy + 224] for dy in range(3)
    )
    for dy in range(3):
        lhs[:, dy * 128 : dy * 128 + 128] = lat[16 * dy : 16 * dy + 224]
    lhs[:, 384:512] = side.astype(BF)

    sum_one = jnp.zeros((8, CH), F32)
    sum_two = jnp.zeros((8, CH), F32)
    for o in range(8):
        out = mm(lhs[48:176, :], wb[:, o * CH : (o + 1) * CH]) + inb[...]
        first[3:11, o] = out.reshape(8, 16, CH)
        own = out.reshape(16, 8, CH)
        sum_one = sum_one + jnp.sum(own, axis=0)
        sum_two = sum_two + jnp.sum(own * own, axis=0)

    def pack(buf, rows):
        for n, row in enumerate(rows):
            row = jnp.sum(row, axis=0, keepdims=True)
            for k in range(4):
                buf[j, n * 4 + k : n * 4 + k + 1, :] = row[:, k * 128 : k * 128 + 128]

    def exchange(phase, buf):
        copies = []
        offsets = ((2, 0), (2, 1), (1, 0), (3, 0), (1, 1), (3, 1), (0, 1))
        for d, (dy, dc) in enumerate(offsets):
            copies.append(
                pltpu.make_async_remote_copy(
                    src_ref=buf.at[j], dst_ref=buf.at[j],
                    send_sem=ex_s.at[phase, d], recv_sem=ex_r.at[phase, d],
                    device_id={"tok": lax.rem(y + dy, 4) * 2 + zh, "grp": lax.rem(c + dc, 2)},
                    device_id_type=MESH,
                )
            )
        for copy in copies:
            copy.start()
        return copies

    def collect(buf, copies):
        for copy in copies:
            copy.wait_recv()
        total = buf[0]
        for k in range(1, 8):
            total = total + buf[k]
        return total

    def as_row(tile, start):
        rowbuf[...] = tile
        return jnp.concatenate([rowbuf[start + k : start + k + 1, :] for k in range(4)], axis=1)

    pack(p1, (sum_one, sum_two))
    ex1 = exchange(0, p1)
    beside = jnp.concatenate([lhs[0:48, :], lhs[176:224, :]], axis=0)
    for o in range(8):
        out = (mm(beside, wb[:, o * CH : (o + 1) * CH]) + inb[...]).reshape(6, 16, CH)
        first[0:3, o] = out[0:3]
        first[11:14, o] = out[3:6]

    stats = group_total(collect(p1, ex1)) / GROUP_N
    mu = as_row(stats, 0)
    rstd = lax.rsqrt(as_row(stats, 4) - mu * mu + EPS)
    coef_a = rstd * gain[...] * 0.5
    coef_b = (nbias[...] - mu * rstd * gain[...]) * 0.5

    blk16 = iota((16, CH), 0)

    def put_row(buf, r, value):
        buf[r, 1:9] = value.astype(BF)
        buf[r, 0] = jnp.where(blk16 > 0, pltpu.roll(value[7], 1, 0), 0.0).astype(BF)
        buf[r, 9] = jnp.where(blk16 < 15, pltpu.roll(value[0], 15, 0), 0.0).astype(BF)

    def inside(row):
        return ((row >= 0) & (row < 64)).astype(F32)

    def act_rows(rows):
        for r in rows:
            half_u = first[r] * coef_a + coef_b
            put_row(act, r, half_u * (1.0 + jnp.tanh(half_u)) * inside(8 * j - 3 + r))

    act_rows((2, 3, 4, 5))

    loads[11].wait()

    def decode(pieces):
        total = None
        for dy in range(3):
            for dx in range(3):
                part = [act[r + dy : r + dy + n, dx : dx + 8].reshape(n * 128, CH) for r, n in pieces]
                part = part[0] if len(part) == 1 else jnp.concatenate(part, axis=0)
                term = mm(part, midk[dy, dx])
                total = term if total is None else total + term
        half_u = (total + midb[...]) * 0.5
        tanh = jnp.tanh(half_u)
        grad = 0.5 * ((1.0 + tanh) + half_u * (1.0 - tanh * tanh))
        return half_u * (1.0 + tanh), grad

    pooled_sum = jnp.zeros((8, CH), F32)
    for i in range(4):
        r = 2 + 2 * i
        act_rows(((6, 7), (8, 9), (10, 11), (0, 1, 12, 13))[i])
        value, grad = decode([(r, 2)])
        slope[r : r + 2] = grad.reshape(2, 8, 16, CH)
        pixel = mm_nt(rgbt, value.astype(BF))
        for colour in range(3):
            for row in range(2):
                at = colour * 8 + 2 * i + row
                pixg[zh, j, at : at + 1, :] = pixel[colour : colour + 1, row * 128 : row * 128 + 128]
        pooled_sum = pooled_sum + jnp.sum(value.reshape(32, 8, CH), axis=0)

    pack(p2, (pooled_sum,))
    ex2 = exchange(1, p2)

    pix_copies = []
    for d in range(1, 16):
        n = lax.rem(tok * 2 + c + d, 16)
        pix_copies.append(
            pltpu.make_async_remote_copy(
                src_ref=pixg.at[zh, j], dst_ref=pixg.at[zh, j],
                send_sem=pix_s.at[d - 1], recv_sem=pix_r.at[d - 1],
                device_id={"tok": lax.div(n, 2), "grp": lax.rem(n, 2)}, device_id_type=MESH,
            )
        )

    for r in range(10):
        half_u = first[r + 2] * coef_a + coef_b
        tanh = jnp.tanh(half_u)
        outer[r] = ((1.0 + tanh) + half_u * (1.0 - tanh * tanh)) * (gain[...] * 0.5)
    _, grad = decode([(0, 2), (10, 2)])
    slope[0:2] = grad[:256].reshape(2, 8, 16, CH)
    slope[10:12] = grad[256:].reshape(2, 8, 16, CH)

    loads[12].wait()
    loads[13].wait()
    target = text[pl.ds(zh, 1), :]
    norm_t = jnp.sqrt(jnp.sum(target * target, axis=-1, keepdims=True) + EPS)
    pooled = (as_row(collect(p2, ex2), 0) / CELLS).astype(BF)
    feature = mm(jnp.broadcast_to(pooled, (8, CH)), clip[...])
    norm_f = jnp.sqrt(jnp.sum(feature * feature, axis=-1, keepdims=True) + EPS)
    reward = jnp.sum(feature * target, axis=-1, keepdims=True) / (norm_f * norm_t)
    grad_feature = (
        REWARD_W * (target / (norm_f * norm_t) - reward * feature / (norm_f * norm_f))
    ).astype(BF)
    grad_act = mm_nt(grad_feature, clip[...])[0:1, :]
    rewb[zh] = jnp.broadcast_to(reward, (8, 128))
    rew_copy = pltpu.make_async_remote_copy(
        src_ref=rewb.at[zh], dst_ref=rewb.at[zh], send_sem=rew_s, recv_sem=rew_r,
        device_id={"tok": y * 2 + 1 - zh}, device_id_type=MESH,
    )
    rew_copy.start()

    def grad_rows(rows):
        for r in rows:
            put_row(gsec, r, slope[r] * grad_act * inside(8 * j - 2 + r))

    grad_rows((1, 2, 3, 4))

    xh_b = mu * rstd

    def back(pieces):
        total = None
        for dy in range(3):
            for dx in range(3):
                part = [
                    gsec[r + 2 - dy : r + 2 - dy + n, 2 - dx : 10 - dx].reshape(n * 128, CH)
                    for r, n in pieces
                ]
                part = part[0] if len(part) == 1 else jnp.concatenate(part, axis=0)
                term = mm_nt(part, midk[dy, dx])
                total = term if total is None else total + term
        def rows_of(buf, shift):
            part = [buf[r + shift : r + shift + n].reshape(n * 128, CH) for r, n in pieces]
            return part[0] if len(part) == 1 else jnp.concatenate(part, axis=0)

        return total * rows_of(outer, 0), rows_of(first, 2) * rstd - xh_b

    sums = [jnp.zeros((8, CH), F32)] * 2
    for i in range(4):
        r = 1 + 2 * i
        grad_rows(((5, 6), (7, 8), (9, 10), (0, 11))[i])
        w, xhat = back([(r, 2)])
        for copy in pix_copies[4 * i : 4 * i + 4]:
            copy.start()
        wgr[r : r + 2] = w.reshape(2, 8, 16, CH)
        sums[0] = sums[0] + jnp.sum(w.reshape(32, 8, CH), axis=0)
        sums[1] = sums[1] + jnp.sum((w * xhat).reshape(32, 8, CH), axis=0)
    pack(p3, sums)
    ex3 = exchange(2, p3)
    w, _ = back([(0, 1), (9, 1)])
    wgr[0:1] = w[:128].reshape(1, 8, 16, CH)
    wgr[9:10] = w[128:].reshape(1, 8, 16, CH)

    stats = group_total(collect(p3, ex3)) / GROUP_N
    mean_w = as_row(stats, 0)
    mean_x = as_row(stats, 4)
    coef_f = -rstd * rstd * mean_x
    coef_0 = (xh_b * mean_x - mean_w) * rstd

    row = 8 * j - 1 + (iota((160, 1), 0) >> 4)
    keep_row = ((row >= 0) & (row < 64)).astype(F32)
    back_y = None
    for o in range(8):
        value = wgr[:, o].reshape(160, CH) * rstd + first[2:12, o].reshape(160, CH) * coef_f
        value = ((value + coef_0) * keep_row).astype(BF)
        term = mm_nt(value, wb[:, o * CH : (o + 1) * CH])
        back_y = term if back_y is None else back_y + term
    grad_lat = jnp.zeros((128, 128), F32)
    edge = jnp.zeros((128, 128), F32)
    lane = iota((128, 128), 1)
    blk = iota((128, 128), 0) & 15
    for dy in range(3):
        start = (2 - dy) * 16
        grad_lat = grad_lat + back_y[start : start + 128, dy * 128 : dy * 128 + 128]
        part = back_y[start : start + 128, 384:512]
        part = jnp.where((lane >> 5) == dy, part, 0.0)
        edge = edge + pltpu.roll(part, (112 - 32 * dy) % 128, 1)
    grad_lat = grad_lat + jnp.where((lane >= 112) & (blk < 15), pltpu.roll(edge, 127, 0), 0.0)
    grad_lat = grad_lat + jnp.where((lane < 16) & (blk > 0), pltpu.roll(edge, 1, 0), 0.0)
    sigma = noise_level(time_ref[zh], (128, 128))
    gvx[c] = (-sigma * (grad_lat / LSCALE)).astype(BF).reshape(2, 64, 128)

    gv_pair = pltpu.make_async_remote_copy(
        src_ref=gvx.at[c], dst_ref=gvx.at[c], send_sem=gx_s, recv_sem=gx_r,
        device_id={"grp": 1 - c}, device_id_type=MESH,
    )
    gv_pair.start()

    def gv_copy(e):
        copy = pltpu.make_async_remote_copy(
            src_ref=gvx.at[c, e], dst_ref=gvr.at[zh],
            send_sem=gv_s.at[e], recv_sem=gv_r.at[zh],
            device_id={"tok": y * 2 + c, "grp": e}, device_id_type=MESH,
        )
        return copy, jnp.logical_not((c == zh) & (c == e))

    for e in range(2):
        copy, ok = gv_copy(e)
        pl.when(ok)(copy.start)

    @pl.when(c == zh)
    def _():
        gvr[zh] = gvx[c, c]

    def tokens(parts):
        for a in range(2):
            rows = [
                part[(2 * p + a) * 16 : (2 * p + a) * 16 + 16, :] for part in parts for p in range(2)
            ]
            full = jnp.concatenate(rows, axis=0).astype(F32)
            for chi in range(4):
                ve[a, pl.ds(chi, 64, stride=4), :] = jnp.where(lane_chi == chi, full, 0.0)
        return jnp.concatenate([ve[0], ve[1]], axis=1).astype(BF)

    j_r, k_c = iota((256, 256), 0), iota((256, 256), 1)
    target_lane = j_r & 63
    keep = ((target_lane >> 5) == (k_c >> 7)) & ((target_lane & 31) == (k_c & 31))
    quad = one_hot(keep & ((j_r < 64) | (j_r >= 192)))
    for copy in mod_copies:
        copy.wait_recv()

    def term_of(row):
        grads = mm_nt(tokens([gvx[row, 0], gvx[row, 1]]), quad).astype(BF)
        lanes = pl.ds(pl.multiple_of(row * 256, 256), 256)
        return mm(modp[0:608, lanes], grads[:, :128]) + mm(modp[608:1216, lanes], grads[:, 128:])

    wt[...] = term_of(c) * (1.0 / 2048.0)
    gv_pair.wait_recv()
    wt[...] += term_of(1 - c) * (1.0 / 2048.0)
    for k in range(16):
        s1send[k, 0:32, :] = wt[38 * k : 38 * k + 32, :].astype(BF)
        tail = jnp.concatenate([wt[38 * k + 32 : 38 * k + 38, :], jnp.zeros((10, 128), F32)], axis=0)
        s1send[k, 32:48, :] = tail.astype(BF)
    me_xy = x * 4 + y
    s1 = []
    offsets = [(dx, dy) for dx in range(4) for dy in range(4) if dx or dy]
    offsets.sort(key=lambda o: -min(o[0], 4 - o[0]) - min(o[1], 4 - o[1]))
    for d, (dx, dy) in enumerate(offsets):
        to_x, to_y = lax.rem(x + dx, 4), lax.rem(y + dy, 4)
        s1.append(
            pltpu.make_async_remote_copy(
                src_ref=s1send.at[to_x * 4 + to_y], dst_ref=s1recv.at[me_xy],
                send_sem=s1_s.at[d], recv_sem=s1_r.at[d],
                device_id={"batch": zl * 4 + to_x, "tok": to_y * 2 + zh}, device_id_type=MESH,
            )
        )
    for copy in s1:
        copy.start()
    s1recv[me_xy] = s1send[me_xy]

    for h in range(2):
        copy = pltpu.make_async_remote_copy(
            src_ref=gvx.at[0, 0], dst_ref=gvr.at[h],
            send_sem=gv_s.at[0], recv_sem=gv_r.at[h],
            device_id={"tok": y * 2 + c, "grp": 0}, device_id_type=MESH,
        )
        pl.when(jnp.logical_not((c == zh) & (zh == h)))(copy.wait_recv)
    own_tokens[...] = tokens([gvr[0], gvr[1]])

    def hidden_rows(i, carry):
        img, start = lax.div(i, 4), pl.multiple_of(lax.rem(i, 4) * 32, 32)
        flat = pl.multiple_of(i * 32, 32)
        grad_mod = mm(own_tokens[pl.ds(flat, 32), :], wrep[...])
        inv = stat_i[pl.ds(flat, 32), :]
        normal = (hid[img, pl.ds(start, 32), :].astype(F32) - stat_m[pl.ds(flat, 32), :]) * inv
        e = grad_mod * (1.0 + scalev[pl.ds(img, 1), :])
        mean_e = jnp.sum(e, axis=-1, keepdims=True) / D
        mean_n = jnp.sum(e * normal, axis=-1, keepdims=True) / D
        hgv[img, pl.ds(start, 32), :] = (inv * (e - mean_e - normal * mean_n)).astype(BF)
        return carry

    lax.fori_loop(0, 8, hidden_rows, 0)

    for copy in s1:
        copy.wait_recv()
    total = s1recv[0].astype(F32)
    for k in range(1, 16):
        total = total + s1recv[k].astype(F32)
    wt[0:48, :] = total
    for z in range(2):
        s2send[z] = wt[19 * z : 19 * z + 24, :]
    me_z = zl * 2 + zh

    def line_copy(n):
        dest_zl, dest_zh, dest_c = 2 * c + n // 4, (n // 2) % 2, n % 2
        copy = pltpu.make_async_remote_copy(
            src_ref=s2send.at[dest_zh], dst_ref=s2recv.at[me_z],
            send_sem=s2_s.at[n], recv_sem=s2_r.at[me_z],
            device_id={"batch": dest_zl * 4 + x, "tok": y * 2 + dest_zh, "grp": dest_c},
            device_id_type=MESH,
        )
        return copy, jnp.logical_not((dest_zl == zl) & (dest_zh == zh) & (dest_c == c))

    for n in range(8):
        copy, ok = line_copy(n)
        pl.when(ok)(copy.start)
    self_line = lax.div(zl, 2) == c

    @pl.when(self_line)
    def _():
        s2recv[me_z] = s2send[zh]

    for copy in pix_copies:
        copy.wait_recv()
    l384, k384 = iota((384, 384), 0), iota((384, 384), 1)
    cell = l384 & 127
    place = jnp.where(k384 == ((cell & 15) * 8 + (cell >> 4)) * 3 + (l384 >> 7), 1.0, 0.0)
    for i in range(2):
        slab = map_ref[i]
        block = pixg[i, slab >> 1]
        odd = jnp.full((24, 128), slab & 1, jnp.int32) == 1
        block = jnp.where(odd, pltpu.roll(block, 20, 0), block)
        wide = jnp.concatenate([block[0:8], block[8:16], block[16:24]], axis=1)
        moved = lax.dot_general(
            wide, place, (((1,), (0,)), ((), ())),
            precision=lax.Precision.HIGHEST, preferred_element_type=F32,
        )
        pix_out[i, 0] = moved[0:4]

    rew_copy.wait_recv()
    lane = iota((1, 128), 1)
    rew_out[...] = jnp.where(lane == 0, rewb[0, 0:1, :], rewb[1, 0:1, :])[:, 0:2]

    for h in range(2):
        for copy, ok in lat_copies(h):
            pl.when(ok)(copy.wait_send)
    for copy in ex1 + ex2 + ex3 + pix_copies + s1 + mod_copies + [rew_copy, gv_pair]:
        copy.wait_send()
    for e in range(2):
        copy, ok = gv_copy(e)
        pl.when(ok)(copy.wait_send)
    for n in range(8):
        copy = pltpu.make_async_remote_copy(
            src_ref=s2send.at[0], dst_ref=s2recv.at[n],
            send_sem=s2_s.at[0], recv_sem=s2_r.at[n],
            device_id={"grp": 1 - c}, device_id_type=MESH,
        )
        pl.when(jnp.logical_not(self_line & (me_z == n)))(copy.wait_recv)
    total = s2recv[0]
    for k in range(1, 8):
        total = total + s2recv[k]
    odd = jnp.full((24, 128), lax.rem(zl, 2), jnp.int32) == 1
    total = jnp.where(odd, pltpu.roll(total, 64, 1), total)
    wg_ref[...] = total[0:19, 0:64]

    for n in range(8):
        copy, ok = line_copy(n)
        pl.when(ok)(copy.wait_send)


def hand_out(*refs):
    sem = refs[8]
    pairs = [(refs[i], refs[4 + i]) for i in range(1, 4)]
    for h in range(2):
        for k in range(4):
            rows = pl.ds(k * 32, 32)
            pairs.append((refs[0].at[h, rows, :], refs[4].at[h, rows, :]))
    copies = [pltpu.make_async_copy(src, dst, sem.at[i]) for i, (src, dst) in enumerate(pairs)]
    for copy in copies:
        copy.start()
    for copy in copies:
        copy.wait()


def local(
    hidden, shift, scale, out_weight, noisy_latent, timestep, in_kernel, in_bias,
    norm_gain, norm_bias, mid_kernel, mid_bias, rgb_weight, clip_weight, text_embed, slab_map,
):
    any_spec = pl.BlockSpec(memory_space=pl.ANY)
    smem = pl.BlockSpec(memory_space=pltpu.SMEM)
    vmem = pl.BlockSpec(memory_space=pltpu.VMEM)
    dma = pltpu.SemaphoreType.DMA

    def v(dtype, *shape):
        return pltpu.VMEM(shape, dtype)

    hg, wg, reward, pixels = pl.pallas_call(
        kernel,
        out_shape=(
            pltpu.VMEM((2, 128, D), BF),
            pltpu.VMEM((19, 64), F32),
            pltpu.VMEM((1, 2), F32),
            pltpu.VMEM((2, 1, 4, 384), F32),
        ),
        in_specs=[smem, smem] + [any_spec] * 14,
        out_specs=(vmem, vmem, vmem, vmem),
        scratch_shapes=[
            v(BF, 2, 128, D), v(F32, 2, D), v(F32, 2, D), v(BF, 64, D), v(F32, 2, 4, 2048),
            v(BF, 3, 3, 16, CH), v(F32, 1, CH), v(F32, 1, CH), v(F32, 1, CH),
            v(BF, 3, 3, CH, CH), v(F32, 1, CH), v(BF, 3, CH), v(BF, CH, EMB), v(F32, 2, EMB),
            v(F32, 256, 1), v(F32, 256, 1), v(BF, 256, D), v(BF, 2, D, 128), v(BF, D // 2, 512),
            v(BF, 256, D), v(F32, 2, 256, 128), v(F32, 2, 4, 16, 128), v(BF, 2, 64, 128),
            v(BF, 4, 64, 128), v(BF, 224, 512), v(BF, 512, 8 * CH),
            v(F32, 14, 8, 16, CH), v(BF, 14, 10, 16, CH), v(F32, 12, 8, 16, CH),
            v(BF, 12, 10, 16, CH), v(F32, 10, 8, 16, CH), v(F32, 10, 8, 16, CH), v(F32, 8, 128),
            v(F32, 8, 8, 128), v(F32, 8, 8, 128), v(F32, 8, 8, 128), v(F32, 2, 8, 128),
            v(F32, 2, 8, 24, 128), v(BF, 2, 2, 64, 128), v(BF, 2, 64, 128), v(F32, 608, 128),
            v(BF, 16, 48, 128), v(BF, 16, 48, 128), v(F32, 2, 24, 128), v(F32, 8, 24, 128),
            v(BF, 256, 256),
            dma((14,)), dma((4,)), dma((4,)), dma((3, 7)), dma((3, 7)), dma((15,)), dma((15,)),
            dma, dma, dma((2, 3)), dma((2, 3)), dma, dma, dma((2,)), dma((2,)), dma((15,)), dma((15,)), dma((8,)), dma((8,)),
        ],
        compiler_params=pltpu.CompilerParams(
            collective_id=0, has_side_effects=True, vmem_limit_bytes=58 * 2**20
        ),
    )(
        timestep, slab_map.reshape(2), hidden, shift, scale, out_weight.T, noisy_latent, in_kernel,
        in_bias.reshape(1, CH), norm_gain.reshape(1, CH), norm_bias.reshape(1, CH),
        mid_kernel, mid_bias.reshape(1, CH), rgb_weight.T, clip_weight, text_embed,
    )
    hg, wg, reward, pixels = pl.pallas_call(
        hand_out,
        out_shape=(
            jax.ShapeDtypeStruct((2, 128, D), BF),
            jax.ShapeDtypeStruct((19, 64), F32),
            jax.ShapeDtypeStruct((1, 2), F32),
            jax.ShapeDtypeStruct((2, 1, 4, 384), F32),
        ),
        in_specs=[vmem] * 4,
        out_specs=[any_spec] * 4,
        scratch_shapes=[dma((11,))],
    )(*[pltpu.with_memory_space_constraint(out, pltpu.VMEM) for out in (hg, wg, reward, pixels)])
    return hg, wg, reward.reshape(2), pixels


def solution(mesh):
    rows = ("tok", "grp")
    return jax.shard_map(
        local,
        mesh=mesh,
        in_specs=(
            P("batch", rows, None), P("batch", None), P("batch", None), P(),
            P("batch", rows, None), P("batch"), P(), P(), P(), P(), P(), P(), P(), P(),
            P("batch", None), P("batch", rows),
        ),
        out_specs=(
            P("batch", rows, None), P(("batch", "tok"), None), P("batch"),
            P("batch", rows, None, None),
        ),
        check_vma=False,
    )
```
